512 devices in a mesh: cluster: 64 (over z, y), panel: 8 (over x, core).
Axes of the slice: x: 4, y: 8, z: 8, core: 2. Of those that a mesh axis runs over, the one named last changes fastest.
Arguments:
- inputs: bfloat16 [256, 65536], P('panel', 'cluster'), may hold values from -6 to 6
- local_order: int32 [65536], P('cluster'), may hold values from 0 to 1023, as said below
- run_counts: int32 [64], replicated, may hold values from 1 to 32, 1024 in all
- near_cols: int32 [4096], P('cluster'), may hold values from 0 to 1023, as said below
- near_blocks: bfloat16 [64, 262144], P(None, 'cluster'), may hold values from -0.25 to 0.25
- near_scales: float32 [4096], P('cluster'), may hold values from 0.25 to 4
- leaf_bases: bfloat16 [16, 65536], P(None, 'cluster'), may hold values from -0.75 to 0.75
- local_tiles: float32 [1920, 16, 16], P('cluster')
- cross_tiles: float32 [120, 16, 16], replicated
Outputs:
- near_field: bfloat16 [256, 65536], P('panel', 'cluster')
- top_coeffs: float32 [64, 16, 256], P('cluster', None, 'panel')
- top_factor: float32 [64, 16, 16], P('cluster')
- top_gram: float32 [64, 16, 16], P('cluster')
The draws below stay inside these ranges and needn't reach their ends.
Inputs may be any that keep to these rules, and one draw needn't show every extreme that they name: `local_order`: each device's 1024 entries are a permutation of 0 .. 1023. `run_counts`: they sum to 1024; the largest is exactly 32. `near_cols`: blocks stand 4 to a row leaf in the order of the row leaves; the first block of a row leaf is its diagonal block; every column leaf lies within 2 leaves of its row leaf.
All inputs are finite; a program needn't handle non-finite values.
Results may differ from the reference program's by a relative error of at most 0.0006.
Values may be sent and summed in bfloat16 or wider, within the bound.
A program may use at most 64 MiB of HBM per device.

```python
import math
import jax
import jax.numpy as jnp
import numpy as np
from jax import lax

LEAF = 64
RANK = 16
COLS = 256
NEAR = 4
REACH = 2
CROSS = 4
LEAVES_DEV = 16
RUNS = 64
PTS_DEV = 1024
NPTS = 65536
NLEAF = 1024
NBLK = 4096
CAP = 32
CROSS_TILES = 120


def draw_local_order(key, part):
    key = jax.random.fold_in(key, 11)
    keys = jax.random.split(key, NPTS // PTS_DEV)
    perms = jax.vmap(lambda single: jax.random.permutation(single, PTS_DEV))(keys)
    return perms.reshape(-1).astype(jnp.int32)


def draw_near_cols(key, part):
    key = jax.random.fold_in(key, 12)
    first, second = jax.random.split(key)
    rows = jnp.arange(NLEAF, dtype=jnp.int32)
    signs = jax.random.randint(first, (NLEAF,), 0, 2) * 2 - 1
    others = jax.random.randint(second, (NLEAF, NEAR - 2), -REACH, REACH + 1)
    offsets = jnp.concatenate([jnp.zeros((NLEAF, 1), jnp.int32), (signs * REACH)[:, None].astype(jnp.int32), others.astype(jnp.int32)], axis=1)
    cols = jnp.clip(rows[:, None] + offsets, 0, NLEAF - 1)
    return cols.reshape(-1).astype(jnp.int32)


def shape_tiles(noise, amount):
    eye = jnp.eye(RANK, dtype=jnp.float32)[None, :, :]
    return (0.7071 * (eye + amount * noise / RANK ** 0.5)).astype(jnp.float32)


def draw_local_tiles(key, part):
    key = jax.random.fold_in(key, 13)
    count = RUNS * (2 * LEAVES_DEV - 2)
    noise = jax.random.normal(key, (count, RANK, RANK), jnp.float32)
    return shape_tiles(noise, 0.3)


def draw_cross_tiles(key, part):
    key = jax.random.fold_in(key, 14)
    noise = jax.random.normal(key, (CROSS_TILES, RANK, RANK), jnp.float32)
    return shape_tiles(noise, 0.3)


def level_of(key, dims, cuts, low, largest):
    gain, own = 1.0, jax.random.fold_in(key, 6)
    for axis_at, shards_of in cuts:
        heights = jnp.exp(jax.random.uniform(jax.random.fold_in(own, axis_at), (shards_of,), jnp.float32, low / len(cuts), largest / len(cuts)))
        gain = gain * jnp.repeat(heights, dims[axis_at] // shards_of).reshape([-1 if axis == axis_at else 1 for axis in range(len(dims))])
    return gain


def split_up(count, total, limit, lean):
    weights = [(1 << 20) // math.isqrt(grade ** lean) + 1 for grade in range(2, count + 1)]
    rest, given = total - limit - (count - 1), [1] * (count - 1)
    while rest > 0:
        free = [i for i in range(count - 1) if given[i] < limit]
        mass, remaining = sum([weights[i] for i in free]), rest
        for i in free:
            extra = min(limit - given[i], max(1, remaining * weights[i] // mass), rest)
            given[i] = given[i] + extra
            rest = rest - extra
    return np.array([limit] + given)


def ragged(stream_key, count, total, reach, skew):
    if count == 2:
        one = jax.random.randint(stream_key, (), max(1, total - reach), min(reach, total - 1) + 1)
        return jnp.stack([one, total - one])
    sizes = jnp.asarray(split_up(count, total, reach, skew), jnp.int32)
    twos = (count - 1) // 2
    giver, taker = sizes[1:1 + 2 * twos:2], sizes[2:2 + 2 * twos:2]
    margin = jnp.minimum(giver - 1, reach - taker)
    passed = jax.random.randint(jax.random.fold_in(stream_key, 1), (twos,), 0, 1 << 20) % (margin + 1)
    sizes = sizes.at[1:1 + 2 * twos:2].set(giver - passed).at[2:2 + 2 * twos:2].set(taker + passed)
    return sizes[jax.random.permutation(jax.random.fold_in(stream_key, 2), count)]


def scatter_about(rng, dims, width, bound, cuts=(), held_as=jnp.bfloat16):
    result = jax.random.normal(rng, dims, jnp.float32) * width
    if len(cuts) > 0:
        result = level_of(rng, dims, cuts, -0.22, 0.18) * result
    return jnp.clip(result, min=-bound, max=bound).astype(held_as)


def setup_inputs(seed: int = 0) -> dict:
    arg_keys = jax.random.split(jax.random.key(seed), 10)
    return {
        "inputs": scatter_about(arg_keys[0], (COLS, NPTS), 1.0, 6.0, ((0, 8), (1, 64))),
        "local_order": draw_local_order(jax.random.fold_in(arg_keys[9], 71), 0),
        "run_counts": ragged(arg_keys[2], RUNS, PTS_DEV, CAP, 2).astype(jnp.int32),
        "near_cols": draw_near_cols(jax.random.fold_in(arg_keys[9], 71), 0),
        "near_blocks": scatter_about(arg_keys[4], (LEAF, NBLK * LEAF), (LEAF * NEAR * 2) ** -0.5, 0.25, ((1, 64),)),
        "near_scales": jnp.clip(jnp.exp(math.log(4.0) - 2.7725887 * jax.random.uniform(arg_keys[5], (NBLK,), jnp.float32) ** level_of(arg_keys[5], (NBLK,), ((0, 64),), -0.2, 0.2)), 0.25, 4.0),
        "leaf_bases": scatter_about(arg_keys[6], (RANK, NPTS), LEAF ** -0.5, 0.75, ((1, 64),)),
        "local_tiles": draw_local_tiles(jax.random.fold_in(arg_keys[9], 71), 0),
        "cross_tiles": draw_cross_tiles(jax.random.fold_in(arg_keys[9], 71), 0),
    }


HIGH = lax.Precision.HIGHEST

def run_table(run_counts, points):
    ends = jnp.cumsum(run_counts)
    starts = ends - run_counts
    position = jnp.arange(points, dtype=jnp.int32)
    runs = jnp.sum((ends[None, :] <= position[:, None]).astype(jnp.int32), axis=1)
    picks = (runs[:, None] == jnp.arange(run_counts.shape[0], dtype=jnp.int32)[None, :]).astype(jnp.int32)
    within = position - jnp.sum(picks * starts[None, :], axis=1)
    return (runs, within)

def flip(mats):
    return jnp.swapaxes(mats, -1, -2)

def merge_nodes(left_r, left_c, right_r, right_c, left_e, right_e):
    left_a = jnp.matmul(left_r, left_e, precision=HIGH)
    right_a = jnp.matmul(right_r, right_e, precision=HIGH)
    gram = jnp.matmul(flip(left_a), left_a, precision=HIGH) + jnp.matmul(flip(right_a), right_a, precision=HIGH)
    moments = jnp.matmul(flip(left_a), left_c, precision=HIGH) + jnp.matmul(flip(right_a), right_c, precision=HIGH)
    lower = jnp.linalg.cholesky(gram)
    coeffs = jax.scipy.linalg.solve_triangular(lower, moments, lower=True)
    return (flip(lower), coeffs)

def reference(inputs, local_order, run_counts, near_cols, near_blocks, near_scales, leaf_bases, local_tiles, cross_tiles):
    runs, within = run_table(run_counts, PTS_DEV)
    dest = jnp.arange(RUNS, dtype=jnp.int32)[:, None]
    source = (dest - runs[None, :]) % RUNS
    order = local_order.reshape(RUNS, PTS_DEV)
    spots = jnp.broadcast_to(jnp.arange(PTS_DEV, dtype=jnp.int32)[None, :], (RUNS, PTS_DEV))
    rows = (source * PTS_DEV + order[source, spots]).astype(jnp.int32)
    relaid = inputs[:, rows.reshape(-1)]
    leaves_all = relaid.reshape(COLS, NLEAF, LEAF)
    blocks = near_blocks.reshape(LEAF, RUNS, LEAVES_DEV * NEAR, LEAF).transpose(1, 0, 2, 3)

    def near_part(pieces):
        cols, mats, scales = pieces
        gathered = leaves_all[:, cols, :].astype(jnp.float32)
        prod = jnp.einsum('kbc,cbr->kbr', gathered, mats.astype(jnp.float32), precision=HIGH)
        prod = prod * scales[None, :, None]
        return prod.reshape(COLS, LEAVES_DEV, NEAR, LEAF).sum(axis=2).reshape(COLS, PTS_DEV)
    parts = lax.map(near_part, (near_cols.reshape(RUNS, LEAVES_DEV * NEAR), blocks, near_scales.reshape(RUNS, LEAVES_DEV * NEAR)))
    near_field = parts.transpose(1, 0, 2).reshape(COLS, NPTS).astype(jnp.bfloat16)
    bases = leaf_bases.reshape(RANK, NLEAF, LEAF).astype(jnp.float32)
    cols_f = leaves_all.astype(jnp.float32)
    gram = jnp.einsum('knp,jnp->nkj', bases, bases, precision=HIGH)
    moments = jnp.einsum('knp,cnp->nkc', bases, cols_f, precision=HIGH)
    lower = jnp.linalg.cholesky(gram)
    factor = flip(lower)
    coeffs = jax.scipy.linalg.solve_triangular(lower, moments, lower=True)
    tiles = local_tiles.reshape(RUNS, 2 * LEAVES_DEV - 2, RANK, RANK)
    count = LEAVES_DEV
    offset = 0
    while count > 1:
        level = tiles[:, offset:offset + count].reshape(RUNS * count, RANK, RANK)
        factor, coeffs = merge_nodes(factor[0::2], coeffs[0::2], factor[1::2], coeffs[1::2], level[0::2], level[1::2])
        offset += count
        count //= 2
    for level_index in range(CROSS):
        total = RUNS // 2 ** level_index
        start = 2 * RUNS - 2 * RUNS // 2 ** level_index
        level = cross_tiles[start:start + total]
        factor, coeffs = merge_nodes(factor[0::2], coeffs[0::2], factor[1::2], coeffs[1::2], level[0::2], level[1::2])
    top_factor = jnp.repeat(factor, 2 ** CROSS, axis=0)
    top_coeffs = jnp.repeat(coeffs, 2 ** CROSS, axis=0)
    top_gram = jnp.matmul(top_coeffs, flip(top_coeffs), precision=HIGH)
    return (near_field, top_coeffs, top_factor, top_gram)
```

```python
import functools

import jax
import jax.numpy as jnp
from jax import lax
from jax.experimental import pallas as pl
from jax.experimental.pallas import tpu as pltpu
from jax.sharding import PartitionSpec as P

LEAF = 64
RANK = 16
NEAR = 4
REACH = 2
CROSS = 4
CAP = 32
LANES = 128
MESH = pl.DeviceIdType.MESH
HIGH = lax.Precision.HIGHEST
F32 = jnp.float32
BF16 = jnp.bfloat16


def iota(shape, dim):
    return lax.broadcasted_iota(jnp.int32, shape, dim)


def dot(a, b, precision=None):
    return lax.dot_general(
        a, b, (((1,), (0,)), ((), ())), precision=precision, preferred_element_type=F32
    )


def dot_t(a, b, precision=None):
    return lax.dot_general(
        a, b, (((1,), (1,)), ((), ())), precision=precision, preferred_element_type=F32
    )


def split3(x):
    hi = x.astype(BF16)
    rest = x - hi.astype(F32)
    mid = rest.astype(BF16)
    low = (rest - mid.astype(F32)).astype(BF16)
    return hi, mid, low


def group_sum(x, width):
    shift = LANES // 2
    while shift >= width:
        x = x + pltpu.roll(x, shift, 1)
        shift //= 2
    return x


def pack2(x):
    keep = iota((RANK, LANES), 0) % 8 == iota((RANK, LANES), 1) // RANK
    return jnp.where(keep, x, 0.0).reshape(2, 8, LANES).sum(axis=1)


def unpack2(x):
    rows = jnp.concatenate(
        [jnp.broadcast_to(x[0:1], (8, LANES)), jnp.broadcast_to(x[1:2], (8, LANES))], axis=0
    )
    keep = iota((RANK, LANES), 0) % 8 == iota((RANK, LANES), 1) // RANK
    return group_sum(jnp.where(keep, rows, 0.0), RANK)


def body(
    devices, panels, x_ref, order_ref, counts_ref, countv_ref, cols_ref, scales_ref, mats_hbm,
    bases_ref, local_hbm, cross_hbm, near_ref, coeffs_ref, factor_ref, topgram_ref,
    mats, local_v, cross_v, sorted_ref, out, recv, own, ext, moment_out, moment_in, gram_out, gram_in,
    top_out, top_in, hot_ref, quarter_ref,
    mats_sem, local_sem, cross_sem, a2a_send, a2a_recv, gram_send, gram_recv, moment_send, moment_recv,
    top_send, top_recv, left_send, left_recv, right_send, right_recv,
):
    me = lax.axis_index("cluster")
    panel = lax.axis_index("panel")
    group = 2**CROSS
    rank_in = lax.rem(me, group)
    base = me - rank_in
    channels, points = x_ref.shape
    leaves = points // LEAF

    load_mats = pltpu.make_async_copy(mats_hbm, mats, mats_sem)
    load_local = pltpu.make_async_copy(local_hbm, local_v, local_sem)
    load_cross = pltpu.make_async_copy(cross_hbm, cross_v, cross_sem)
    load_local.start()
    load_cross.start()
    load_mats.start()

    barrier = pltpu.get_barrier_semaphore()

    def greet(m, carry):
        pl.semaphore_signal(
            barrier, 1, device_id=(lax.rem(me + m, devices), panel), device_id_type=MESH
        )
        return carry

    lax.fori_loop(1, devices, greet, 0, unroll=9)

    def greet_panel(m, carry):
        pl.semaphore_signal(
            barrier, 1, device_id=(me, lax.rem(panel + m, panels)), device_id_type=MESH
        )
        return carry

    lax.fori_loop(1, panels, greet_panel, 0, unroll=7)

    x4 = jnp.concatenate([x_ref[...]] * 4, axis=0)
    point = iota((LANES, points), 1)
    hots = []
    for b in range(points // LANES):
        row = jnp.broadcast_to(order_ref[b : b + 1, :], (LANES, LANES))
        col = jnp.concatenate([row.T] * (points // LANES), axis=1)
        hots.append((col == point).astype(F32).astype(BF16))
    sorted_ref[pl.ds(0, points), :] = dot_t(jnp.concatenate(hots, axis=0), x4)
    sorted_ref[pl.ds(points, CAP), :] = jnp.zeros((CAP, LANES), F32)

    part = iota((8, LANES), 1) // channels

    def fill(m, start):
        rows = [sorted_ref[pl.ds(start + 8 * q, 8), :] for q in range(4)]
        low = jnp.where(part == 0, rows[0], rows[1])
        high = jnp.where(part == 2, rows[2], rows[3])
        out[m] = jnp.where(part < 2, low, high).astype(BF16)
        return start + counts_ref[m]

    lax.fori_loop(0, devices, fill, 0, unroll=8)

    pl.semaphore_wait(barrier, devices - 1 + panels - 1)

    def send(m, carry):
        pltpu.make_async_remote_copy(
            out.at[m], recv.at[m], a2a_send, a2a_recv,
            device_id=(lax.rem(me + m, devices), panel), device_id_type=MESH,
        ).start()
        return carry

    lax.fori_loop(1, devices, send, 0, unroll=9)
    recv[0] = out[0]

    load_local.wait()
    load_cross.wait()
    tiles = local_v.shape[2]
    lane = iota((tiles, LANES), 1)
    leaf = lane % leaves
    want = jnp.where(
        lane < leaves, leaf,
        jnp.where(
            lane < 2 * leaves, 16 + leaf // 2,
            jnp.where(lane < 3 * leaves, 24 + leaf // 4, 28 + leaf // 8),
        ),
    )
    pick_local = ((iota((tiles, LANES), 0) == want) & (lane < 4 * leaves)).astype(F32).astype(BF16)
    tiles_x = cross_v.shape[2]
    lane = iota((tiles_x, LANES), 1)
    level = lane // leaves - 4
    firsts = [2 * devices - 2 * devices // 2**t + me // 2**t for t in range(CROSS)]
    want = jnp.where(
        level == 0, firsts[0],
        jnp.where(level == 1, firsts[1], jnp.where(level == 2, firsts[2], firsts[3])),
    )
    pick_cross = ((iota((tiles_x, LANES), 0) == want) & (level >= 0)).astype(F32).astype(BF16)
    chain = jnp.zeros((RANK * RANK, LANES), F32)
    for source, pick in ((local_v, pick_local), (cross_v, pick_cross)):
        flat = source[...].reshape(RANK * RANK, source.shape[2])
        for term in split3(flat):
            chain = chain + dot(term, pick)
    for step in (leaves, 2 * leaves, 4 * leaves):
        left = chain.reshape(RANK, RANK, LANES)
        right = pltpu.roll(chain, LANES - step, 1).reshape(RANK, RANK, LANES)
        total = left[:, 0:1, :] * right[0:1]
        for k in range(1, RANK):
            total = total + left[:, k : k + 1, :] * right[k : k + 1]
        chain = total.reshape(RANK * RANK, LANES)
    hi, mid, low = split3(chain)
    lane = iota((RANK * RANK, LANES), 1)
    terms = jnp.where(
        lane < leaves, hi.astype(F32),
        jnp.where(
            lane < 2 * leaves, pltpu.roll(mid.astype(F32), leaves, 1),
            jnp.where(lane < 3 * leaves, pltpu.roll(low.astype(F32), 2 * leaves, 1), 0.0),
        ),
    ).astype(BF16)
    spread = iota((LANES, points), 0)
    spread = ((spread % leaves == iota((LANES, points), 1) // LEAF) & (spread < 3 * leaves))
    path = dot(terms, spread.astype(F32).astype(BF16)).reshape(RANK, RANK, points)
    bases = bases_ref[...].astype(F32)
    weights = path[0] * bases[0:1]
    for k in range(1, RANK):
        weights = weights + path[k] * bases[k : k + 1]
    parts = split3(weights)
    weights3 = jnp.concatenate(parts, axis=0)

    wide = jnp.concatenate([p for p in parts for _ in range(8)], axis=0)
    gram = dot_t(weights3, wide)
    gram = gram[0:RANK] + gram[RANK : 2 * RANK] + gram[2 * RANK :]
    gram = gram[:, 0:LANES] + gram[:, LANES : 2 * LANES] + gram[:, 2 * LANES :]
    packed = pack2(gram)
    gram_out[...] = packed
    gram_in[rank_in] = packed

    def send_gram(m, carry):
        pltpu.make_async_remote_copy(
            gram_out, gram_in.at[rank_in], gram_send, gram_recv,
            device_id=(base + lax.rem(rank_in + m, group), panel), device_id_type=MESH,
        ).start()
        return carry

    lax.fori_loop(1, group, send_gram, 0, unroll=15)

    counts = countv_ref[...].astype(F32)
    square = (devices, devices)
    upto = (iota(square, 0) <= iota(square, 1)).astype(F32).astype(BF16)
    ends = dot(jnp.broadcast_to(counts, (8, devices)).astype(BF16), upto)[0:1]
    diagonal = jnp.where(iota(square, 0) == iota(square, 1), jnp.broadcast_to(counts, square), 0.0)
    counts_col = dot(diagonal.astype(BF16), jnp.ones((devices, LANES), BF16))
    both = jnp.concatenate([counts_col, jnp.ones((devices, LANES), F32)], axis=1).astype(BF16)
    position = iota((points, devices), 0).astype(F32)
    passed = dot((ends <= position).astype(F32).astype(BF16), both)
    within = (iota((points, LANES), 0).astype(F32) - passed[:, :LANES]).astype(jnp.int32)
    run = passed[:, LANES:].astype(jnp.int32)
    quarter_ref[...] = (within // 8 == iota((points, LANES), 1) // channels).astype(F32)
    slot = run * 8 + within % 8
    slots = devices * 8
    hot_ref[...] = (
        (jnp.concatenate([slot] * (slots // LANES), axis=1) == iota((points, slots), 1))
        .astype(F32)
        .astype(BF16)
    )

    others = pl.ds(1, devices - 1)
    pltpu.make_async_copy(recv.at[others], recv.at[others], a2a_recv).wait()

    received = recv[...].astype(F32).reshape(slots, LANES).astype(BF16)
    relaid = dot(hot_ref[...], received)
    relaid = jnp.where(quarter_ref[...] > 0.5, relaid, 0.0).astype(BF16)

    moment = dot(weights3, relaid)
    moment = moment[0:RANK] + moment[RANK : 2 * RANK] + moment[2 * RANK :]
    moment = group_sum(moment, channels)
    part = iota((4, LANES), 1) // channels
    low = jnp.where(part == 0, moment[0:4], moment[4:8])
    high = jnp.where(part == 2, moment[8:12], moment[12:16])
    packed = jnp.where(part < 2, low, high)
    moment_out[...] = packed
    moment_in[rank_in] = packed

    def send_moment(m, carry):
        pltpu.make_async_remote_copy(
            moment_out, moment_in.at[rank_in], moment_send, moment_recv,
            device_id=(base + lax.rem(rank_in + m, group), panel), device_id_type=MESH,
        ).start()
        return carry

    lax.fori_loop(1, group, send_moment, 0, unroll=15)

    fold = (iota((channels, LANES), 1) % channels == iota((channels, LANES), 0)).astype(F32).astype(BF16)
    for n in range(leaves):
        columns = dot_t(fold, relaid[n * LEAF : (n + 1) * LEAF]).astype(BF16)
        own[n] = columns
        ext[n + REACH] = columns
    right = lax.rem(me + 1, devices)
    left = lax.rem(me + devices - 1, devices)
    to_left = pltpu.make_async_remote_copy(
        own.at[pl.ds(0, REACH)], ext.at[pl.ds(leaves + REACH, REACH)], left_send, left_recv,
        device_id=(left, panel), device_id_type=MESH,
    )
    to_right = pltpu.make_async_remote_copy(
        own.at[pl.ds(leaves - REACH, REACH)], ext.at[pl.ds(0, REACH)], right_send, right_recv,
        device_id=(right, panel), device_id_type=MESH,
    )
    to_left.start()
    to_right.start()

    peers = pl.ds(0, group - 1)
    pltpu.make_async_copy(gram_in.at[peers], gram_in.at[peers], gram_recv).wait()
    sub = iota((RANK, LANES), 0)
    lane = iota((RANK, LANES), 1)
    tableau = jnp.where(
        lane < RANK, unpack2(jnp.sum(gram_in[...], axis=0)), (lane - RANK == sub).astype(F32)
    )
    for k in range(RANK - 1):
        ratio = tableau[:, k : k + 1] / tableau[k : k + 1, k : k + 1]
        tableau = tableau - jnp.where(sub > k, ratio * tableau[k : k + 1, :], 0.0)
    pivots = jnp.sum(jnp.where(lane == sub, tableau, 0.0), axis=1, keepdims=True)
    tableau = tableau * (1.0 / jnp.sqrt(pivots))
    factor_ref[0] = jnp.where(lane >= sub, tableau, 0.0)[:, :RANK]
    inverse = tableau[:, RANK : 2 * RANK]

    load_mats.wait()

    def near_leaf(i, source, first):
        rows = jnp.concatenate(
            [source[jnp.clip(cols_ref[NEAR * i + t] - first, 0, source.shape[0] - 1)] for t in range(NEAR)],
            axis=0,
        )
        width = NEAR * LEAF
        prod = dot(rows, mats[:, i * width : (i + 1) * width])
        lower = iota((channels, LANES), 1) < LEAF
        halves = []
        for h in range(2):
            cut = prod[:, h * LANES : (h + 1) * LANES]
            halves.append(
                jnp.where(
                    lower,
                    cut[2 * h * channels : (2 * h + 1) * channels] * scales_ref[NEAR * i + 2 * h],
                    cut[(2 * h + 1) * channels : (2 * h + 2) * channels] * scales_ref[NEAR * i + 2 * h + 1],
                )
            )
        both = halves[0] + halves[1]
        return both + pltpu.roll(both, LEAF, 1)

    def near_pair(i, source, first):
        a = near_leaf(i, source, first)
        b = near_leaf(i + 1, source, first)
        lower = iota((channels, LANES), 1) < LEAF
        near_ref[:, i * LEAF : (i + 2) * LEAF] = jnp.where(lower, a, b).astype(BF16)

    for i in range(REACH, leaves - REACH, 2):
        near_pair(i, own, me * leaves)

    pltpu.make_async_copy(moment_in.at[peers], moment_in.at[peers], moment_recv).wait()
    packed = jnp.sum(moment_in[...], axis=0)
    moment = jnp.concatenate(
        [packed[:, q * channels : (q + 1) * channels] for q in range(4)], axis=0
    )
    coeffs = dot(inverse, moment, HIGH)
    coeffs_ref[0] = coeffs
    packed = pack2(dot_t(coeffs, jnp.concatenate([coeffs] * 8, axis=0), HIGH))
    top_out[...] = packed
    top_in[panel] = packed

    def send_top(m, carry):
        pltpu.make_async_remote_copy(
            top_out, top_in.at[panel], top_send, top_recv,
            device_id=(me, lax.rem(panel + m, panels)), device_id_type=MESH,
        ).start()
        return carry

    lax.fori_loop(1, panels, send_top, 0, unroll=7)

    to_left.wait_recv()
    to_right.wait_recv()
    first = me * leaves - REACH
    near_pair(0, ext, first)
    near_pair(leaves - 2, ext, first)

    peers = pl.ds(0, panels - 1)
    pltpu.make_async_copy(top_in.at[peers], top_in.at[peers], top_recv).wait()
    topgram_ref[0] = unpack2(jnp.sum(top_in[...], axis=0))[:, :RANK]

    pltpu.make_async_copy(out.at[others], out.at[others], a2a_send).wait()
    peers = pl.ds(0, group - 1)
    pltpu.make_async_copy(gram_in.at[peers], gram_in.at[peers], gram_send).wait()
    pltpu.make_async_copy(moment_in.at[peers], moment_in.at[peers], moment_send).wait()
    peers = pl.ds(0, panels - 1)
    pltpu.make_async_copy(top_in.at[peers], top_in.at[peers], top_send).wait()
    to_left.wait_send()
    to_right.wait_send()


def on_device(
    inputs, local_order, run_counts, near_cols, near_blocks, near_scales, leaf_bases, local_tiles,
    cross_tiles,
):
    devices = lax.axis_size("cluster")
    panels = lax.axis_size("panel")
    channels, points = inputs.shape
    leaves = points // LEAF
    group = 2**CROSS
    vmem = pl.BlockSpec(memory_space=pltpu.VMEM)
    smem = pl.BlockSpec(memory_space=pltpu.SMEM)
    hbm = pl.BlockSpec(memory_space=pl.ANY)
    local_t = jnp.transpose(local_tiles, (1, 2, 0))
    cross_t = jnp.transpose(cross_tiles, (1, 2, 0))
    dma = pltpu.SemaphoreType.DMA
    return pl.pallas_call(
        functools.partial(body, devices, panels),
        out_shape=(
            jax.ShapeDtypeStruct((channels, points), BF16),
            jax.ShapeDtypeStruct((1, RANK, channels), F32),
            jax.ShapeDtypeStruct((1, RANK, RANK), F32),
            jax.ShapeDtypeStruct((1, RANK, RANK), F32),
        ),
        in_specs=[vmem, vmem, smem, vmem, smem, smem, hbm, vmem, hbm, hbm],
        out_specs=(vmem, vmem, vmem, vmem),
        scratch_shapes=[
            pltpu.VMEM(near_blocks.shape, BF16),
            pltpu.VMEM(local_t.shape, F32),
            pltpu.VMEM(cross_t.shape, F32),
            pltpu.VMEM((points + CAP, LANES), F32),
            pltpu.VMEM((devices, 8, LANES), BF16),
            pltpu.VMEM((devices, 8, LANES), BF16),
            pltpu.VMEM((leaves, channels, LEAF), BF16),
            pltpu.VMEM((leaves + 2 * REACH, channels, LEAF), BF16),
            pltpu.VMEM((4, LANES), F32),
            pltpu.VMEM((group, 4, LANES), F32),
            pltpu.VMEM((2, LANES), F32),
            pltpu.VMEM((group, 2, LANES), F32),
            pltpu.VMEM((2, LANES), F32),
            pltpu.VMEM((panels, 2, LANES), F32),
            pltpu.VMEM((points, devices * 8), BF16),
            pltpu.VMEM((points, LANES), F32),
        ]
        + [dma] * 15,
        compiler_params=pltpu.CompilerParams(
            collective_id=0, has_side_effects=True, vmem_limit_bytes=48 * 2**20
        ),
    )(
        inputs,
        local_order.reshape(points // LANES, LANES),
        run_counts,
        run_counts.reshape(1, devices),
        near_cols,
        near_scales,
        near_blocks,
        leaf_bases,
        local_t,
        cross_t,
    )


def solution(mesh):
    placed = (
        P("panel", "cluster"),
        P("cluster"),
        P(),
        P("cluster"),
        P(None, "cluster"),
        P("cluster"),
        P(None, "cluster"),
        P("cluster", None, None),
        P(),
    )
    return jax.shard_map(
        on_device,
        mesh=mesh,
        in_specs=placed,
        out_specs=(
            P("panel", "cluster"),
            P("cluster", None, "panel"),
            P("cluster", None, None),
            P("cluster", None, None),
        ),
        check_vma=False,
    )
```

```python
import functools

import jax
import jax.numpy as jnp
from jax import lax
from jax.experimental import pallas as pl
from jax.experimental.pallas import tpu as pltpu
from jax.sharding import PartitionSpec as P

LEAF = 64
RANK = 16
NEAR = 4
REACH = 2
CROSS = 4
CAP = 32
SIDE = 8
LANES = 128
MESH = pl.DeviceIdType.MESH
HIGH = lax.Precision.HIGHEST
F32 = jnp.float32
BF16 = jnp.bfloat16


def iota(shape, dim):
    return lax.broadcasted_iota(jnp.int32, shape, dim)


def dot(a, b, precision=None):
    return lax.dot_general(
        a, b, (((1,), (0,)), ((), ())), precision=precision, preferred_element_type=F32
    )


def dot_t(a, b, precision=None):
    return lax.dot_general(
        a, b, (((1,), (1,)), ((), ())), precision=precision, preferred_element_type=F32
    )


def split3(x):
    hi = x.astype(BF16)
    rest = x - hi.astype(F32)
    mid = rest.astype(BF16)
    low = (rest - mid.astype(F32)).astype(BF16)
    return hi, mid, low


def group_sum(x, width):
    shift = LANES // 2
    while shift >= width:
        x = x + pltpu.roll(x, shift, 1)
        shift //= 2
    return x


def pack2(x):
    keep = iota((RANK, LANES), 0) % 8 == iota((RANK, LANES), 1) // RANK
    return jnp.where(keep, x, 0.0).reshape(2, 8, LANES).sum(axis=1)


def unpack2(x):
    rows = jnp.concatenate(
        [jnp.broadcast_to(x[0:1], (8, LANES)), jnp.broadcast_to(x[1:2], (8, LANES))], axis=0
    )
    keep = iota((RANK, LANES), 0) % 8 == iota((RANK, LANES), 1) // RANK
    return group_sum(jnp.where(keep, rows, 0.0), RANK)


def body(
    devices, panels, x_hbm, order_hbm, counts_hbm, countv_hbm, cols_hbm, scales_hbm, mats_hbm,
    bases_hbm, local_hbm, cross_hbm, near_ref, coeffs_ref, factor_ref, topgram_ref,
    x_ref, order_ref, counts_ref, countv_ref, cols_ref, scales_ref, mats, bases_ref, local_v, cross_v,
    sorted_ref, out, middle, recv, own, ext, moment_out, moment_in, gram_out, gram_in,
    top_out, top_in, hot_ref, quarter_ref,
    load_sems, one_send, one_recv, two_send, two_recv, gram_send, gram_recv, moment_send, moment_recv,
    top_send, top_recv, left_send, left_recv, right_send, right_recv,
):
    me = lax.axis_index("cluster")
    panel = lax.axis_index("panel")
    group = 2**CROSS
    rank_in = lax.rem(me, group)
    base = me - rank_in
    channels, points = x_ref.shape
    leaves = points // LEAF

    rows = devices // SIDE
    y = lax.rem(me, SIDE)
    z = me // SIDE
    y_first = 1 - lax.rem(panel, 2)
    z_first = 1 - y_first

    def load(source, target, at):
        copy = pltpu.make_async_copy(source, target, load_sems.at[at])
        copy.start()
        return copy

    load_x = load(x_hbm, x_ref, 0)
    load_order = load(order_hbm, order_ref, 1)
    load_counts = load(counts_hbm, counts_ref, 2)
    load_local = load(local_hbm, local_v, 3)
    load_cross = load(cross_hbm, cross_v, 4)
    load_bases = load(bases_hbm, bases_ref, 5)
    load_countv = load(countv_hbm, countv_ref, 6)
    load_cols = load(cols_hbm, cols_ref, 7)
    load_scales = load(scales_hbm, scales_ref, 8)
    load_mats = load(mats_hbm, mats, 9)

    barrier = pltpu.get_barrier_semaphore()

    def at(dz, dy):
        return lax.rem(z + dz, rows) * SIDE + lax.rem(y + dy, SIDE)

    for k in range(1, SIDE):
        pl.semaphore_signal(barrier, 1, device_id=(at(0, k), panel), device_id_type=MESH)
    for k in range(1, rows):
        pl.semaphore_signal(barrier, 1, device_id=(at(k, 0), panel), device_id_type=MESH)
    for k in range(1, panels):
        pl.semaphore_signal(
            barrier, 1, device_id=(me, lax.rem(panel + k, panels)), device_id_type=MESH
        )

    load_x.wait()
    load_order.wait()
    x4 = jnp.concatenate([x_ref[...]] * 4, axis=0)
    point = iota((LANES, points), 1)
    hots = []
    for b in range(points // LANES):
        row = jnp.broadcast_to(order_ref[b : b + 1, :], (LANES, LANES))
        col = jnp.concatenate([row.T] * (points // LANES), axis=1)
        hots.append((col == point).astype(F32).astype(BF16))
    sorted_ref[pl.ds(0, points), :] = dot_t(jnp.concatenate(hots, axis=0), x4)
    sorted_ref[pl.ds(points, CAP), :] = jnp.zeros((CAP, LANES), F32)

    load_counts.wait()
    part = iota((8, LANES), 1) // channels

    def fill(m, start):
        cuts = [sorted_ref[pl.ds(start + 8 * q, 8), :] for q in range(4)]
        low = jnp.where(part == 0, cuts[0], cuts[1])
        high = jnp.where(part == 2, cuts[2], cuts[3])
        dy = lax.rem(m, SIDE)
        dz = lax.rem(m // SIDE + (y + dy) // SIDE, rows)
        out[y_first * dy + z_first * dz, y_first * dz + z_first * dy] = jnp.where(
            part < 2, low, high
        ).astype(BF16)
        return start + counts_ref[m]

    lax.fori_loop(0, devices, fill, 0, unroll=8)

    pl.semaphore_wait(barrier, SIDE - 1 + rows - 1 + panels - 1)

    one = [
        pltpu.make_async_remote_copy(
            out.at[k], middle.at[k], one_send, one_recv,
            device_id=(at(z_first * k, y_first * k), panel), device_id_type=MESH,
        )
        for k in range(1, SIDE)
    ]
    for copy in one:
        copy.start()
    middle[0] = out[0]

    load_local.wait()
    load_cross.wait()
    tiles = local_v.shape[2]
    lane = iota((tiles, LANES), 1)
    leaf = lane % leaves
    want = jnp.where(
        lane < leaves, leaf,
        jnp.where(
            lane < 2 * leaves, 16 + leaf // 2,
            jnp.where(lane < 3 * leaves, 24 + leaf // 4, 28 + leaf // 8),
        ),
    )
    pick_local = ((iota((tiles, LANES), 0) == want) & (lane < 4 * leaves)).astype(F32).astype(BF16)
    tiles_x = cross_v.shape[2]
    lane = iota((tiles_x, LANES), 1)
    level = lane // leaves - 4
    firsts = [2 * devices - 2 * devices // 2**t + me // 2**t for t in range(CROSS)]
    want = jnp.where(
        level == 0, firsts[0],
        jnp.where(level == 1, firsts[1], jnp.where(level == 2, firsts[2], firsts[3])),
    )
    pick_cross = ((iota((tiles_x, LANES), 0) == want) & (level >= 0)).astype(F32).astype(BF16)
    chain = jnp.zeros((RANK * RANK, LANES), F32)
    for source, pick in ((local_v, pick_local), (cross_v, pick_cross)):
        flat = source[...].reshape(RANK * RANK, source.shape[2])
        for term in split3(flat):
            chain = chain + dot(term, pick)
    for step in (leaves, 2 * leaves, 4 * leaves):
        left = chain.reshape(RANK, RANK, LANES)
        right = pltpu.roll(chain, LANES - step, 1).reshape(RANK, RANK, LANES)
        total = left[:, 0:1, :] * right[0:1]
        for k in range(1, RANK):
            total = total + left[:, k : k + 1, :] * right[k : k + 1]
        chain = total.reshape(RANK * RANK, LANES)
    hi, mid, low = split3(chain)
    lane = iota((RANK * RANK, LANES), 1)
    terms = jnp.where(
        lane < leaves, hi.astype(F32),
        jnp.where(
            lane < 2 * leaves, pltpu.roll(mid.astype(F32), leaves, 1),
            jnp.where(lane < 3 * leaves, pltpu.roll(low.astype(F32), 2 * leaves, 1), 0.0),
        ),
    ).astype(BF16)
    spread = iota((LANES, points), 0)
    spread = ((spread % leaves == iota((LANES, points), 1) // LEAF) & (spread < 3 * leaves))
    path = dot(terms, spread.astype(F32).astype(BF16)).reshape(RANK, RANK, points)
    load_bases.wait()
    bases = bases_ref[...].astype(F32)
    weights = path[0] * bases[0:1]
    for k in range(1, RANK):
        weights = weights + path[k] * bases[k : k + 1]
    parts = split3(weights)
    weights3 = jnp.concatenate(parts, axis=0)

    wide = jnp.concatenate([p for p in parts for _ in range(8)], axis=0)
    gram = dot_t(weights3, wide)
    gram = gram[0:RANK] + gram[RANK : 2 * RANK] + gram[2 * RANK :]
    gram = gram[:, 0:LANES] + gram[:, LANES : 2 * LANES] + gram[:, 2 * LANES :]
    packed = pack2(gram)
    gram_out[...] = packed
    gram_in[rank_in] = packed

    load_countv.wait()
    counts = countv_ref[...].astype(F32)
    square = (devices, devices)
    upto = (iota(square, 0) <= iota(square, 1)).astype(F32).astype(BF16)
    ends = dot(jnp.broadcast_to(counts, (8, devices)).astype(BF16), upto)[0:1]
    diagonal = jnp.where(iota(square, 0) == iota(square, 1), jnp.broadcast_to(counts, square), 0.0)
    counts_col = dot(diagonal.astype(BF16), jnp.ones((devices, LANES), BF16))
    both = jnp.concatenate([counts_col, jnp.ones((devices, LANES), F32)], axis=1).astype(BF16)
    position = iota((points, devices), 0).astype(F32)
    passed = dot((ends <= position).astype(F32).astype(BF16), both)
    within = (iota((points, LANES), 0).astype(F32) - passed[:, :LANES]).astype(jnp.int32)
    run = passed[:, LANES:].astype(jnp.int32)
    quarter_ref[...] = (within // 8 == iota((points, LANES), 1) // channels).astype(F32)
    dy = run % SIDE
    dz = (run // SIDE + (dy > y).astype(jnp.int32)) % rows
    slot = (y_first * (dz * SIDE + dy) + z_first * (dy * rows + dz)) * 8 + within % 8
    slots = devices * 8
    hot_ref[...] = (
        (jnp.concatenate([slot] * (slots // LANES), axis=1) == iota((points, slots), 1))
        .astype(F32)
        .astype(BF16)
    )

    others = pl.ds(1, SIDE - 1)
    pltpu.make_async_copy(middle.at[others], middle.at[others], one_recv).wait()
    two = [
        pltpu.make_async_remote_copy(
            middle.at[:, k], recv.at[k], two_send, two_recv,
            device_id=(at(y_first * k, z_first * k), panel), device_id_type=MESH,
        )
        for k in range(1, SIDE)
    ]
    for copy in two:
        copy.start()
    recv[0] = middle[:, 0]

    def send_gram(m, carry):
        pltpu.make_async_remote_copy(
            gram_out, gram_in.at[rank_in], gram_send, gram_recv,
            device_id=(base + lax.rem(rank_in + m, group), panel), device_id_type=MESH,
        ).start()
        return carry

    lax.fori_loop(1, group, send_gram, 0, unroll=15)

    pltpu.make_async_copy(recv.at[others], recv.at[others], two_recv).wait()

    received = recv[...].astype(F32).reshape(slots, LANES).astype(BF16)
    relaid = dot(hot_ref[...], received)
    relaid = jnp.where(quarter_ref[...] > 0.5, relaid, 0.0).astype(BF16)

    moment = dot(weights3, relaid)
    moment = moment[0:RANK] + moment[RANK : 2 * RANK] + moment[2 * RANK :]
    moment = group_sum(moment, channels)
    part = iota((4, LANES), 1) // channels
    low = jnp.where(part == 0, moment[0:4], moment[4:8])
    high = jnp.where(part == 2, moment[8:12], moment[12:16])
    packed = jnp.where(part < 2, low, high)
    moment_out[...] = packed
    moment_in[rank_in] = packed

    def send_moment(m, carry):
        pltpu.make_async_remote_copy(
            moment_out, moment_in.at[rank_in], moment_send, moment_recv,
            device_id=(base + lax.rem(rank_in + m, group), panel), device_id_type=MESH,
        ).start()
        return carry

    lax.fori_loop(1, group, send_moment, 0, unroll=15)

    fold = (iota((channels, LANES), 1) % channels == iota((channels, LANES), 0)).astype(F32).astype(BF16)
    for n in range(leaves):
        columns = dot_t(fold, relaid[n * LEAF : (n + 1) * LEAF]).astype(BF16)
        own[n] = columns
        ext[n + REACH] = columns
    right = lax.rem(me + 1, devices)
    left = lax.rem(me + devices - 1, devices)
    to_left = pltpu.make_async_remote_copy(
        own.at[pl.ds(0, REACH)], ext.at[pl.ds(leaves + REACH, REACH)], left_send, left_recv,
        device_id=(left, panel), device_id_type=MESH,
    )
    to_right = pltpu.make_async_remote_copy(
        own.at[pl.ds(leaves - REACH, REACH)], ext.at[pl.ds(0, REACH)], right_send, right_recv,
        device_id=(right, panel), device_id_type=MESH,
    )
    to_left.start()
    to_right.start()

    peers = pl.ds(0, group - 1)
    pltpu.make_async_copy(gram_in.at[peers], gram_in.at[peers], gram_recv).wait()
    sub = iota((RANK, LANES), 0)
    lane = iota((RANK, LANES), 1)
    tableau = jnp.where(
        lane < RANK, unpack2(jnp.sum(gram_in[...], axis=0)), (lane - RANK == sub).astype(F32)
    )
    for k in range(RANK - 1):
        ratio = tableau[:, k : k + 1] / tableau[k : k + 1, k : k + 1]
        tableau = tableau - jnp.where(sub > k, ratio * tableau[k : k + 1, :], 0.0)
    pivots = jnp.sum(jnp.where(lane == sub, tableau, 0.0), axis=1, keepdims=True)
    tableau = tableau * (1.0 / jnp.sqrt(pivots))
    factor_ref[0] = jnp.where(lane >= sub, tableau, 0.0)[:, :RANK]
    inverse = tableau[:, RANK : 2 * RANK]

    load_cols.wait()
    load_scales.wait()
    load_mats.wait()

    def near_leaf(i, source, first):
        rows = jnp.concatenate(
            [source[jnp.clip(cols_ref[NEAR * i + t] - first, 0, source.shape[0] - 1)] for t in range(NEAR)],
            axis=0,
        )
        width = NEAR * LEAF
        prod = dot(rows, mats[:, i * width : (i + 1) * width])
        lower = iota((channels, LANES), 1) < LEAF
        halves = []
        for h in range(2):
            cut = prod[:, h * LANES : (h + 1) * LANES]
            halves.append(
                jnp.where(
                    lower,
                    cut[2 * h * channels : (2 * h + 1) * channels] * scales_ref[NEAR * i + 2 * h],
                    cut[(2 * h + 1) * channels : (2 * h + 2) * channels] * scales_ref[NEAR * i + 2 * h + 1],
                )
            )
        both = halves[0] + halves[1]
        return both + pltpu.roll(both, LEAF, 1)

    def near_pair(i, source, first):
        a = near_leaf(i, source, first)
        b = near_leaf(i + 1, source, first)
        lower = iota((channels, LANES), 1) < LEAF
        near_ref[:, i * LEAF : (i + 2) * LEAF] = jnp.where(lower, a, b).astype(BF16)

    for i in range(REACH, leaves - REACH, 2):
        near_pair(i, own, me * leaves)

    pltpu.make_async_copy(moment_in.at[peers], moment_in.at[peers], moment_recv).wait()
    packed = jnp.sum(moment_in[...], axis=0)
    moment = jnp.concatenate(
        [packed[:, q * channels : (q + 1) * channels] for q in range(4)], axis=0
    )
    coeffs = dot(inverse, moment, HIGH)
    coeffs_ref[0] = coeffs
    packed = pack2(dot_t(coeffs, jnp.concatenate([coeffs] * 8, axis=0), HIGH))
    top_out[...] = packed
    top_in[panel] = packed

    def send_top(m, carry):
        pltpu.make_async_remote_copy(
            top_out, top_in.at[panel], top_send, top_recv,
            device_id=(me, lax.rem(panel + m, panels)), device_id_type=MESH,
        ).start()
        return carry

    lax.fori_loop(1, panels, send_top, 0, unroll=7)

    to_left.wait_recv()
    to_right.wait_recv()
    first = me * leaves - REACH
    near_pair(0, ext, first)
    near_pair(leaves - 2, ext, first)

    peers = pl.ds(0, panels - 1)
    pltpu.make_async_copy(top_in.at[peers], top_in.at[peers], top_recv).wait()
    topgram_ref[0] = unpack2(jnp.sum(top_in[...], axis=0))[:, :RANK]

    pltpu.make_async_copy(out.at[others], out.at[others], one_send).wait()
    pltpu.make_async_copy(recv.at[others], recv.at[others], two_send).wait()
    peers = pl.ds(0, group - 1)
    pltpu.make_async_copy(gram_in.at[peers], gram_in.at[peers], gram_send).wait()
    pltpu.make_async_copy(moment_in.at[peers], moment_in.at[peers], moment_send).wait()
    peers = pl.ds(0, panels - 1)
    pltpu.make_async_copy(top_in.at[peers], top_in.at[peers], top_send).wait()
    to_left.wait_send()
    to_right.wait_send()


def on_device(
    inputs, local_order, run_counts, near_cols, near_blocks, near_scales, leaf_bases, local_tiles,
    cross_tiles,
):
    devices = lax.axis_size("cluster")
    panels = lax.axis_size("panel")
    channels, points = inputs.shape
    leaves = points // LEAF
    group = 2**CROSS
    vmem = pl.BlockSpec(memory_space=pltpu.VMEM)
    hbm = pl.BlockSpec(memory_space=pl.ANY)
    dma = pltpu.SemaphoreType.DMA
    operands = (
        inputs,
        local_order.reshape(points // LANES, LANES),
        run_counts,
        run_counts.reshape(1, devices),
        near_cols,
        near_scales,
        near_blocks,
        leaf_bases,
        jnp.transpose(local_tiles, (1, 2, 0)),
        jnp.transpose(cross_tiles, (1, 2, 0)),
    )
    operands = [pltpu.with_memory_space_constraint(x, pltpu.HBM) for x in operands]
    spaces = [pltpu.VMEM, pltpu.VMEM, pltpu.SMEM, pltpu.VMEM, pltpu.SMEM, pltpu.SMEM] + [pltpu.VMEM] * 4
    slots = (SIDE, SIDE, 8, LANES)
    shapes = (
        ((channels, points), BF16),
        ((1, RANK, channels), F32),
        ((1, RANK, RANK), F32),
        ((1, RANK, RANK), F32),
    )
    results = pl.pallas_call(
        functools.partial(body, devices, panels),
        out_shape=tuple(pltpu.VMEM(*s) for s in shapes),
        in_specs=[hbm] * len(operands),
        out_specs=(vmem,) * 4,
        scratch_shapes=[space(x.shape, x.dtype) for space, x in zip(spaces, operands)]
        + [
            pltpu.VMEM((points + CAP, LANES), F32),
            pltpu.VMEM(slots, BF16),
            pltpu.VMEM(slots, BF16),
            pltpu.VMEM(slots, BF16),
            pltpu.VMEM((leaves, channels, LEAF), BF16),
            pltpu.VMEM((leaves + 2 * REACH, channels, LEAF), BF16),
            pltpu.VMEM((4, LANES), F32),
            pltpu.VMEM((group, 4, LANES), F32),
            pltpu.VMEM((2, LANES), F32),
            pltpu.VMEM((group, 2, LANES), F32),
            pltpu.VMEM((2, LANES), F32),
            pltpu.VMEM((panels, 2, LANES), F32),
            pltpu.VMEM((points, devices * 8), BF16),
            pltpu.VMEM((points, LANES), F32),
            dma((len(operands),)),
        ]
        + [dma] * 14,
        compiler_params=pltpu.CompilerParams(
            collective_id=0, has_side_effects=True, vmem_limit_bytes=48 * 2**20
        ),
    )(*operands)
    return pl.pallas_call(
        store,
        out_shape=tuple(jax.ShapeDtypeStruct(*s) for s in shapes),
        in_specs=[hbm] * 4,
        out_specs=(hbm,) * 4,
        scratch_shapes=[dma((4,))],
    )(*[pltpu.with_memory_space_constraint(x, pltpu.VMEM) for x in results])


def store(*refs):
    sems = refs[8]
    copies = [pltpu.make_async_copy(refs[k], refs[4 + k], sems.at[k]) for k in range(4)]
    for copy in copies:
        copy.start()
    for copy in copies:
        copy.wait()


def solution(mesh):
    placed = (
        P("panel", "cluster"),
        P("cluster"),
        P(),
        P("cluster"),
        P(None, "cluster"),
        P("cluster"),
        P(None, "cluster"),
        P("cluster", None, None),
        P(),
    )
    return jax.shard_map(
        on_device,
        mesh=mesh,
        in_specs=placed,
        out_specs=(
            P("panel", "cluster"),
            P("cluster", None, "panel"),
            P("cluster", None, None),
            P("cluster", None, None),
        ),
        check_vma=False,
    )
```

```python
import functools

import jax
import jax.numpy as jnp
from jax import lax
from jax.experimental import pallas as pl
from jax.experimental.pallas import tpu as pltpu
from jax.sharding import PartitionSpec as P

LEAF = 64
RANK = 16
NEAR = 4
REACH = 2
CROSS = 4
CAP = 32
SIDE = 8
LANES = 128
MESH = pl.DeviceIdType.MESH
HIGH = lax.Precision.HIGHEST
F32 = jnp.float32
BF16 = jnp.bfloat16


def iota(shape, dim):
    return lax.broadcasted_iota(jnp.int32, shape, dim)


def dot(a, b, precision=None):
    return lax.dot_general(
        a, b, (((1,), (0,)), ((), ())), precision=precision, preferred_element_type=F32
    )


def dot_t(a, b, precision=None):
    return lax.dot_general(
        a, b, (((1,), (1,)), ((), ())), precision=precision, preferred_element_type=F32
    )


def split3(x):
    hi = x.astype(BF16)
    rest = x - hi.astype(F32)
    mid = rest.astype(BF16)
    low = (rest - mid.astype(F32)).astype(BF16)
    return hi, mid, low


def group_sum(x, width):
    shift = LANES // 2
    while shift >= width:
        x = x + pltpu.roll(x, shift, 1)
        shift //= 2
    return x


def pack2(x):
    keep = iota((RANK, LANES), 0) % 8 == iota((RANK, LANES), 1) // RANK
    return jnp.where(keep, x, 0.0).reshape(2, 8, LANES).sum(axis=1)


def unpack2(x):
    rows = jnp.concatenate(
        [jnp.broadcast_to(x[0:1], (8, LANES)), jnp.broadcast_to(x[1:2], (8, LANES))], axis=0
    )
    keep = iota((RANK, LANES), 0) % 8 == iota((RANK, LANES), 1) // RANK
    return group_sum(jnp.where(keep, rows, 0.0), RANK)


def body(
    devices, panels, x_hbm, order_hbm, counts_hbm, countv_hbm, cols_hbm, scales_hbm, mats_hbm,
    bases_hbm, local_hbm, cross_hbm, near_ref, coeffs_ref, factor_ref, topgram_ref,
    x_ref, order_ref, counts_ref, countv_ref, cols_ref, scales_ref, mats, bases_ref, local_v, cross_v,
    sorted_ref, out, middle, recv, weight_out, weight_in, own, ext, moment_out, moment_in, gram_out, gram_in,
    top_out, top_in, hot_ref, quarter_ref,
    load_sems, one_send, one_recv, weight_send, weight_recv, two_send, two_recv, gram_send, gram_recv, moment_send, moment_recv,
    top_send, top_recv, left_send, left_recv, right_send, right_recv,
):
    me = lax.axis_index("cluster")
    panel = lax.axis_index("panel")
    group = 2**CROSS
    rank_in = lax.rem(me, group)
    base = me - rank_in
    channels, points = x_ref.shape
    leaves = points // LEAF

    rows = devices // SIDE
    y = lax.rem(me, SIDE)
    z = me // SIDE

    def load(source, target, at):
        copy = pltpu.make_async_copy(source, target, load_sems.at[at])
        copy.start()
        return copy

    load_x = load(x_hbm, x_ref, 0)
    load_order = load(order_hbm, order_ref, 1)
    load_counts = load(counts_hbm, counts_ref, 2)
    load_local = load(local_hbm, local_v, 3)
    load_cross = load(cross_hbm, cross_v, 4)
    load_bases = load(bases_hbm, bases_ref, 5)
    load_countv = load(countv_hbm, countv_ref, 6)
    load_cols = load(cols_hbm, cols_ref, 7)
    load_scales = load(scales_hbm, scales_ref, 8)
    load_mats = load(mats_hbm, mats, 9)

    barrier = pltpu.get_barrier_semaphore()

    def at(dz, dy):
        return lax.rem(z + dz, rows) * SIDE + lax.rem(y + dy, SIDE)

    for k in range(1, SIDE):
        pl.semaphore_signal(barrier, 1, device_id=(at(0, k), panel), device_id_type=MESH)
    for k in range(1, rows):
        pl.semaphore_signal(barrier, 1, device_id=(at(k, 0), panel), device_id_type=MESH)
    twin = 1 - 2 * lax.rem(z, 2) + rows
    for k in range(1, SIDE):
        pl.semaphore_signal(barrier, 1, device_id=(at(twin, k), panel), device_id_type=MESH)
    for k in range(1, panels):
        pl.semaphore_signal(
            barrier, 1, device_id=(me, lax.rem(panel + k, panels)), device_id_type=MESH
        )

    load_x.wait()
    load_order.wait()
    x4 = jnp.concatenate([x_ref[...]] * 4, axis=0)
    point = iota((LANES, points), 1)
    hots = []
    for b in range(points // LANES):
        row = jnp.broadcast_to(order_ref[b : b + 1, :], (LANES, LANES))
        col = jnp.concatenate([row.T] * (points // LANES), axis=1)
        hots.append((col == point).astype(F32).astype(BF16))
    sorted_ref[pl.ds(0, points), :] = dot_t(jnp.concatenate(hots, axis=0), x4)
    sorted_ref[pl.ds(points, CAP), :] = jnp.zeros((CAP, LANES), F32)

    load_counts.wait()
    part = iota((8, LANES), 1) // channels

    def fill(m, start):
        cuts = [sorted_ref[pl.ds(start + 8 * q, 8), :] for q in range(4)]
        low = jnp.where(part == 0, cuts[0], cuts[1])
        high = jnp.where(part == 2, cuts[2], cuts[3])
        dy = lax.rem(m, SIDE)
        dz = lax.rem(m // SIDE + (y + dy) // SIDE, rows)
        out[dz, dy] = jnp.where(part < 2, low, high).astype(BF16)
        return start + counts_ref[m]

    lax.fori_loop(0, devices, fill, 0, unroll=8)

    load_local.wait()
    load_cross.wait()
    tiles = local_v.shape[2]
    lane = iota((tiles, LANES), 1)
    leaf = lane % leaves
    want = jnp.where(
        lane < leaves, leaf,
        jnp.where(
            lane < 2 * leaves, 16 + leaf // 2,
            jnp.where(lane < 3 * leaves, 24 + leaf // 4, 28 + leaf // 8),
        ),
    )
    pick_local = ((iota((tiles, LANES), 0) == want) & (lane < 4 * leaves)).astype(F32).astype(BF16)
    tiles_x = cross_v.shape[2]
    lane = iota((tiles_x, LANES), 1)
    level = lane // leaves - 4
    firsts = [2 * devices - 2 * devices // 2**t + me // 2**t for t in range(CROSS)]
    want = jnp.where(
        level == 0, firsts[0],
        jnp.where(level == 1, firsts[1], jnp.where(level == 2, firsts[2], firsts[3])),
    )
    pick_cross = ((iota((tiles_x, LANES), 0) == want) & (level >= 0)).astype(F32).astype(BF16)
    chain = jnp.zeros((RANK * RANK, LANES), F32)
    for source, pick in ((local_v, pick_local), (cross_v, pick_cross)):
        flat = source[...].reshape(RANK * RANK, source.shape[2])
        for term in split3(flat):
            chain = chain + dot(term, pick)
    for step in (leaves, 2 * leaves, 4 * leaves):
        left = chain.reshape(RANK, RANK, LANES)
        right = pltpu.roll(chain, LANES - step, 1).reshape(RANK, RANK, LANES)
        total = left[:, 0:1, :] * right[0:1]
        for k in range(1, RANK):
            total = total + left[:, k : k + 1, :] * right[k : k + 1]
        chain = total.reshape(RANK * RANK, LANES)
    hi, mid, low = split3(chain)
    lane = iota((RANK * RANK, LANES), 1)
    terms = jnp.where(
        lane < leaves, hi.astype(F32),
        jnp.where(
            lane < 2 * leaves, pltpu.roll(mid.astype(F32), leaves, 1),
            jnp.where(lane < 3 * leaves, pltpu.roll(low.astype(F32), 2 * leaves, 1), 0.0),
        ),
    ).astype(BF16)
    spread = iota((LANES, points), 0)
    spread = ((spread % leaves == iota((LANES, points), 1) // LEAF) & (spread < 3 * leaves))
    path = dot(terms, spread.astype(F32).astype(BF16)).reshape(RANK, RANK, points)
    load_bases.wait()
    bases = bases_ref[...].astype(F32)
    weights = path[0] * bases[0:1]
    for k in range(1, RANK):
        weights = weights + path[k] * bases[k : k + 1]
    parts = split3(weights)
    weights3 = jnp.concatenate(parts, axis=0)

    wide = jnp.concatenate([p for p in parts for _ in range(8)], axis=0)
    gram = dot_t(weights3, wide)
    gram = gram[0:RANK] + gram[RANK : 2 * RANK] + gram[2 * RANK :]
    gram = gram[:, 0:LANES] + gram[:, LANES : 2 * LANES] + gram[:, 2 * LANES :]
    packed = pack2(gram)
    gram_out[...] = packed
    gram_in[rank_in] = packed

    pl.semaphore_wait(barrier, 2 * (SIDE - 1) + rows - 1 + panels - 1)

    one = [
        pltpu.make_async_remote_copy(
            out.at[k], middle.at[k], one_send, one_recv,
            device_id=(at(k, 0), panel), device_id_type=MESH,
        )
        for k in range(1, rows)
    ]
    for copy in one:
        copy.start()
    middle[0] = out[0]
    def send_gram(m, carry):
        pltpu.make_async_remote_copy(
            gram_out, gram_in.at[rank_in], gram_send, gram_recv,
            device_id=(base + lax.rem(rank_in + m, group), panel), device_id_type=MESH,
        ).start()
        return carry

    lax.fori_loop(1, group, send_gram, 0, unroll=15)

    load_countv.wait()
    counts = countv_ref[...].astype(F32)
    square = (devices, devices)
    upto = (iota(square, 0) <= iota(square, 1)).astype(F32).astype(BF16)
    ends = dot(jnp.broadcast_to(counts, (8, devices)).astype(BF16), upto)[0:1]
    diagonal = jnp.where(iota(square, 0) == iota(square, 1), jnp.broadcast_to(counts, square), 0.0)
    counts_col = dot(diagonal.astype(BF16), jnp.ones((devices, LANES), BF16))
    both = jnp.concatenate([counts_col, jnp.ones((devices, LANES), F32)], axis=1).astype(BF16)
    position = iota((points, devices), 0).astype(F32)
    passed = dot((ends <= position).astype(F32).astype(BF16), both)
    within = (iota((points, LANES), 0).astype(F32) - passed[:, :LANES]).astype(jnp.int32)
    run = passed[:, LANES:].astype(jnp.int32)
    quarter_ref[...] = (within // 8 == iota((points, LANES), 1) // channels).astype(F32)
    dy = run % SIDE
    dz = (run // SIDE + (dy > y).astype(jnp.int32)) % rows
    slot = (dy * rows + dz) * 8 + within % 8
    slots = devices * 8
    hot_ref[...] = (
        (jnp.concatenate([slot] * (slots // LANES), axis=1) == iota((points, slots), 1))
        .astype(F32)
        .astype(BF16)
    )

    lower = (iota(square, 1) <= iota(square, 0)).astype(F32).astype(BF16)
    ends_col = dot(lower, counts_col.astype(BF16))
    passed_row = (
        (jnp.concatenate([ends_col] * (points // LANES), axis=1) <= iota((devices, points), 1).astype(F32))
        .astype(F32)
        .astype(BF16)
    )
    starts_row = dot(jnp.broadcast_to(counts, (8, devices)).astype(BF16), passed_row)[0:1]
    quarter_row = (iota((1, points), 1).astype(F32) - starts_row).astype(jnp.int32) // 8
    pair = jnp.concatenate([parts[0], parts[1]], axis=0).astype(F32)
    keep = quarter_row == iota((4 * 2 * RANK, points), 0) // (2 * RANK)
    spaced = jnp.where(keep, jnp.concatenate([pair] * 4, axis=0), 0.0).astype(BF16)
    spaced = dot(spaced, hot_ref[...]).T.astype(BF16)
    weight_out[...] = spaced.reshape(SIDE, slots // SIDE, LANES)

    for k in range(1, SIDE):
        pltpu.make_async_remote_copy(
            weight_out.at[k], weight_in.at[k], weight_send, weight_recv,
            device_id=(at(0, SIDE - k), panel), device_id_type=MESH,
        ).start()
    weight_in[0] = weight_out[0]

    others = pl.ds(1, SIDE - 1)
    pltpu.make_async_copy(weight_in.at[others], weight_in.at[others], weight_recv).wait()
    pltpu.make_async_copy(middle.at[others], middle.at[others], one_recv).wait()

    held = jnp.concatenate(
        [middle[:, k].astype(F32).reshape(rows * 8, LANES) for k in range(SIDE)], axis=0
    ).astype(BF16)
    moment = lax.dot_general(
        weight_in[...].reshape(slots, LANES), held, (((0,), (0,)), ((), ())),
        preferred_element_type=F32,
    )
    part = iota((2 * RANK, LANES), 1) // channels
    moment = sum(
        jnp.where(part == q, moment[q * 2 * RANK : (q + 1) * 2 * RANK], 0.0) for q in range(4)
    )
    moment = group_sum(moment[:RANK] + moment[RANK:], channels)
    part = iota((4, LANES), 1) // channels
    low = jnp.where(part == 0, moment[0:4], moment[4:8])
    high = jnp.where(part == 2, moment[8:12], moment[12:16])
    packed = jnp.where(part < 2, low, high)
    moment_out[...] = packed
    moment_in[rank_in] = packed

    def send_moment(m, carry):
        pltpu.make_async_remote_copy(
            moment_out, moment_in.at[rank_in], moment_send, moment_recv,
            device_id=(base + lax.rem(rank_in + m, group), panel), device_id_type=MESH,
        ).start()
        return carry

    lax.fori_loop(1, group, send_moment, 0, unroll=15)

    two = [
        pltpu.make_async_remote_copy(
            middle.at[:, k], recv.at[k], two_send, two_recv,
            device_id=(at(0, k), panel), device_id_type=MESH,
        )
        for k in range(1, SIDE)
    ]
    for copy in two:
        copy.start()
    recv[0] = middle[:, 0]

    peers = pl.ds(0, group - 1)
    pltpu.make_async_copy(gram_in.at[peers], gram_in.at[peers], gram_recv).wait()
    sub = iota((RANK, LANES), 0)
    lane = iota((RANK, LANES), 1)
    tableau = jnp.where(
        lane < RANK, unpack2(jnp.sum(gram_in[...], axis=0)), (lane - RANK == sub).astype(F32)
    )
    for k in range(RANK - 1):
        ratio = tableau[:, k : k + 1] / tableau[k : k + 1, k : k + 1]
        tableau = tableau - jnp.where(sub > k, ratio * tableau[k : k + 1, :], 0.0)
    pivots = jnp.sum(jnp.where(lane == sub, tableau, 0.0), axis=1, keepdims=True)
    tableau = tableau * (1.0 / jnp.sqrt(pivots))
    factor_ref[0] = jnp.where(lane >= sub, tableau, 0.0)[:, :RANK]
    inverse = tableau[:, RANK : 2 * RANK]

    pltpu.make_async_copy(moment_in.at[peers], moment_in.at[peers], moment_recv).wait()
    packed = jnp.sum(moment_in[...], axis=0)
    moment = jnp.concatenate(
        [packed[:, q * channels : (q + 1) * channels] for q in range(4)], axis=0
    )
    coeffs = dot(inverse, moment, HIGH)
    coeffs_ref[0] = coeffs
    packed = pack2(dot_t(coeffs, jnp.concatenate([coeffs] * 8, axis=0), HIGH))
    top_out[...] = packed
    top_in[panel] = packed

    def send_top(m, carry):
        pltpu.make_async_remote_copy(
            top_out, top_in.at[panel], top_send, top_recv,
            device_id=(me, lax.rem(panel + m, panels)), device_id_type=MESH,
        ).start()
        return carry

    lax.fori_loop(1, panels, send_top, 0, unroll=7)

    pltpu.make_async_copy(recv.at[others], recv.at[others], two_recv).wait()

    received = recv[...].astype(F32).reshape(slots, LANES).astype(BF16)
    relaid = dot(hot_ref[...], received)
    relaid = jnp.where(quarter_ref[...] > 0.5, relaid, 0.0).astype(BF16)

    fold = (iota((channels, LANES), 1) % channels == iota((channels, LANES), 0)).astype(F32).astype(BF16)
    for n in range(leaves):
        columns = dot_t(fold, relaid[n * LEAF : (n + 1) * LEAF]).astype(BF16)
        own[n] = columns
        ext[n + REACH] = columns
    right = lax.rem(me + 1, devices)
    left = lax.rem(me + devices - 1, devices)
    to_left = pltpu.make_async_remote_copy(
        own.at[pl.ds(0, REACH)], ext.at[pl.ds(leaves + REACH, REACH)], left_send, left_recv,
        device_id=(left, panel), device_id_type=MESH,
    )
    to_right = pltpu.make_async_remote_copy(
        own.at[pl.ds(leaves - REACH, REACH)], ext.at[pl.ds(0, REACH)], right_send, right_recv,
        device_id=(right, panel), device_id_type=MESH,
    )
    has_left = me > 0
    has_right = me < devices - 1

    @pl.when(has_left)
    def _():
        to_left.start()

    @pl.when(has_right)
    def _():
        to_right.start()

    @pl.when(me == 0)
    def _():
        ext[pl.ds(0, REACH)] = jnp.zeros((REACH, channels, LEAF), BF16)

    @pl.when(me == devices - 1)
    def _():
        ext[pl.ds(leaves + REACH, REACH)] = jnp.zeros((REACH, channels, LEAF), BF16)


    load_cols.wait()
    load_scales.wait()
    load_mats.wait()

    def near_leaf(i, source, first):
        rows = jnp.concatenate(
            [source[jnp.clip(cols_ref[NEAR * i + t] - first, 0, source.shape[0] - 1)] for t in range(NEAR)],
            axis=0,
        )
        width = NEAR * LEAF
        prod = dot(rows, mats[:, i * width : (i + 1) * width])
        lower = iota((channels, LANES), 1) < LEAF
        halves = []
        for h in range(2):
            cut = prod[:, h * LANES : (h + 1) * LANES]
            halves.append(
                jnp.where(
                    lower,
                    cut[2 * h * channels : (2 * h + 1) * channels] * scales_ref[NEAR * i + 2 * h],
                    cut[(2 * h + 1) * channels : (2 * h + 2) * channels] * scales_ref[NEAR * i + 2 * h + 1],
                )
            )
        both = halves[0] + halves[1]
        return both + pltpu.roll(both, LEAF, 1)

    def near_pair(i, source, first):
        a = near_leaf(i, source, first)
        b = near_leaf(i + 1, source, first)
        lower = iota((channels, LANES), 1) < LEAF
        near_ref[:, i * LEAF : (i + 2) * LEAF] = jnp.where(lower, a, b).astype(BF16)

    for i in range(REACH, leaves - REACH, 2):
        near_pair(i, own, me * leaves)

    @pl.when(has_right)
    def _():
        to_left.wait_recv()

    @pl.when(has_left)
    def _():
        to_right.wait_recv()

    first = me * leaves - REACH
    near_pair(0, ext, first)
    near_pair(leaves - 2, ext, first)

    peers = pl.ds(0, panels - 1)
    pltpu.make_async_copy(top_in.at[peers], top_in.at[peers], top_recv).wait()
    topgram_ref[0] = unpack2(jnp.sum(top_in[...], axis=0))[:, :RANK]

    pltpu.make_async_copy(out.at[others], out.at[others], one_send).wait()
    pltpu.make_async_copy(weight_in.at[others], weight_in.at[others], weight_send).wait()
    pltpu.make_async_copy(recv.at[others], recv.at[others], two_send).wait()
    peers = pl.ds(0, group - 1)
    pltpu.make_async_copy(gram_in.at[peers], gram_in.at[peers], gram_send).wait()
    pltpu.make_async_copy(moment_in.at[peers], moment_in.at[peers], moment_send).wait()
    peers = pl.ds(0, panels - 1)
    pltpu.make_async_copy(top_in.at[peers], top_in.at[peers], top_send).wait()
    @pl.when(has_left)
    def _():
        to_left.wait_send()

    @pl.when(has_right)
    def _():
        to_right.wait_send()


def on_device(
    inputs, local_order, run_counts, near_cols, near_blocks, near_scales, leaf_bases, local_tiles,
    cross_tiles,
):
    devices = lax.axis_size("cluster")
    panels = lax.axis_size("panel")
    channels, points = inputs.shape
    leaves = points // LEAF
    group = 2**CROSS
    vmem = pl.BlockSpec(memory_space=pltpu.VMEM)
    hbm = pl.BlockSpec(memory_space=pl.ANY)
    dma = pltpu.SemaphoreType.DMA
    operands = (
        inputs,
        local_order.reshape(points // LANES, LANES),
        run_counts,
        run_counts.reshape(1, devices),
        near_cols,
        near_scales,
        near_blocks,
        leaf_bases,
        jnp.transpose(local_tiles, (1, 2, 0)),
        jnp.transpose(cross_tiles, (1, 2, 0)),
    )
    operands = [pltpu.with_memory_space_constraint(x, pltpu.HBM) for x in operands]
    spaces = [pltpu.VMEM, pltpu.VMEM, pltpu.SMEM, pltpu.VMEM, pltpu.SMEM, pltpu.SMEM] + [pltpu.VMEM] * 4
    slots = (SIDE, SIDE, 8, LANES)
    shapes = (
        ((channels, points), BF16),
        ((1, RANK, channels), F32),
        ((1, RANK, RANK), F32),
        ((1, RANK, RANK), F32),
    )
    results = pl.pallas_call(
        functools.partial(body, devices, panels),
        out_shape=tuple(pltpu.VMEM(*s) for s in shapes),
        in_specs=[hbm] * len(operands),
        out_specs=(vmem,) * 4,
        scratch_shapes=[space(x.shape, x.dtype) for space, x in zip(spaces, operands)]
        + [
            pltpu.VMEM((points + CAP, LANES), F32),
            pltpu.VMEM(slots, BF16),
            pltpu.VMEM(slots, BF16),
            pltpu.VMEM(slots, BF16),
            pltpu.VMEM((SIDE, devices * 8 // SIDE, LANES), BF16),
            pltpu.VMEM((SIDE, devices * 8 // SIDE, LANES), BF16),
            pltpu.VMEM((leaves, channels, LEAF), BF16),
            pltpu.VMEM((leaves + 2 * REACH, channels, LEAF), BF16),
            pltpu.VMEM((4, LANES), F32),
            pltpu.VMEM((group, 4, LANES), F32),
            pltpu.VMEM((2, LANES), F32),
            pltpu.VMEM((group, 2, LANES), F32),
            pltpu.VMEM((2, LANES), F32),
            pltpu.VMEM((panels, 2, LANES), F32),
            pltpu.VMEM((points, devices * 8), BF16),
            pltpu.VMEM((points, LANES), F32),
            dma((len(operands),)),
        ]
        + [dma] * 16,
        compiler_params=pltpu.CompilerParams(
            collective_id=0, has_side_effects=True, vmem_limit_bytes=48 * 2**20
        ),
    )(*operands)
    return pl.pallas_call(
        store,
        out_shape=tuple(jax.ShapeDtypeStruct(*s) for s in shapes),
        in_specs=[hbm] * 4,
        out_specs=(hbm,) * 4,
        scratch_shapes=[dma((4,))],
    )(*[pltpu.with_memory_space_constraint(x, pltpu.VMEM) for x in results])


def store(*refs):
    sems = refs[8]
    copies = [pltpu.make_async_copy(refs[k], refs[4 + k], sems.at[k]) for k in range(4)]
    for copy in copies:
        copy.start()
    for copy in copies:
        copy.wait()


def solution(mesh):
    placed = (
        P("panel", "cluster"),
        P("cluster"),
        P(),
        P("cluster"),
        P(None, "cluster"),
        P("cluster"),
        P(None, "cluster"),
        P("cluster", None, None),
        P(),
    )
    return jax.shard_map(
        on_device,
        mesh=mesh,
        in_specs=placed,
        out_specs=(
            P("panel", "cluster"),
            P("cluster", None, "panel"),
            P("cluster", None, None),
            P("cluster", None, None),
        ),
        check_vma=False,
    )
```

```python
import functools

import jax
import jax.numpy as jnp
from jax import lax
from jax.experimental import pallas as pl
from jax.experimental.pallas import tpu as pltpu
from jax.sharding import PartitionSpec as P

LEAF = 64
RANK = 16
NEAR = 4
REACH = 2
CROSS = 4
CAP = 32
SIDE = 8
LANES = 128
MESH = pl.DeviceIdType.MESH
HIGH = lax.Precision.HIGHEST
F32 = jnp.float32
BF16 = jnp.bfloat16


def iota(shape, dim):
    return lax.broadcasted_iota(jnp.int32, shape, dim)


def dot(a, b, precision=None):
    return lax.dot_general(
        a, b, (((1,), (0,)), ((), ())), precision=precision, preferred_element_type=F32
    )


def dot_t(a, b, precision=None):
    return lax.dot_general(
        a, b, (((1,), (1,)), ((), ())), precision=precision, preferred_element_type=F32
    )


def split3(x):
    hi = x.astype(BF16)
    rest = x - hi.astype(F32)
    mid = rest.astype(BF16)
    low = (rest - mid.astype(F32)).astype(BF16)
    return hi, mid, low


def group_sum(x, width):
    shift = LANES // 2
    while shift >= width:
        x = x + pltpu.roll(x, shift, 1)
        shift //= 2
    return x


def pack2(x):
    keep = iota((RANK, LANES), 0) % 8 == iota((RANK, LANES), 1) // RANK
    return jnp.where(keep, x, 0.0).reshape(2, 8, LANES).sum(axis=1)


def unpack2(x):
    rows = jnp.concatenate(
        [jnp.broadcast_to(x[0:1], (8, LANES)), jnp.broadcast_to(x[1:2], (8, LANES))], axis=0
    )
    keep = iota((RANK, LANES), 0) % 8 == iota((RANK, LANES), 1) // RANK
    return group_sum(jnp.where(keep, rows, 0.0), RANK)


def body(
    devices, panels, x_hbm, order_hbm, counts_hbm, countv_hbm, cols_hbm, scales_hbm, mats_hbm,
    bases_hbm, local_hbm, cross_hbm, near_ref, coeffs_ref, factor_ref, topgram_ref,
    x_ref, order_ref, counts_ref, countv_ref, cols_ref, scales_ref, mats, bases_ref, local_v, cross_v,
    sorted_ref, out, middle, recv, weight_out, weight_in, own, ext, moment_out, moment_in, gram_out, gram_in,
    top_out, top_in, hot_ref, quarter_ref,
    load_sems, one_send, one_recv, weight_send, weight_recv, two_send, two_recv, gram_send, gram_recv, moment_send, moment_recv,
    top_send, top_recv, left_send, left_recv, right_send, right_recv,
):
    me = lax.axis_index("cluster")
    panel = lax.axis_index("panel")
    group = 2**CROSS
    rank_in = lax.rem(me, group)
    channels, points = x_ref.shape
    leaves = points // LEAF

    rows = devices // SIDE
    y = lax.rem(me, SIDE)
    z = me // SIDE

    def load(source, target, at):
        copy = pltpu.make_async_copy(source, target, load_sems.at[at])
        copy.start()
        return copy

    load_x = load(x_hbm, x_ref, 0)
    load_order = load(order_hbm, order_ref, 1)
    load_counts = load(counts_hbm, counts_ref, 2)
    load_local = load(local_hbm, local_v, 3)
    load_cross = load(cross_hbm, cross_v, 4)
    load_bases = load(bases_hbm, bases_ref, 5)
    load_countv = load(countv_hbm, countv_ref, 6)
    load_cols = load(cols_hbm, cols_ref, 7)
    load_scales = load(scales_hbm, scales_ref, 8)
    load_mats = load(mats_hbm, mats, 9)

    barrier = pltpu.get_barrier_semaphore()

    def at(dz, dy):
        return lax.rem(z + dz, rows) * SIDE + lax.rem(y + dy, SIDE)

    far = sorted(range(1, SIDE), key=lambda k: -min(k, SIDE - k))
    for k in far:
        pl.semaphore_signal(barrier, 1, device_id=(at(k, 0), panel), device_id_type=MESH)
    for k in far:
        pl.semaphore_signal(barrier, 1, device_id=(at(0, k), panel), device_id_type=MESH)
    twin = 1 - 2 * lax.rem(z, 2) + rows
    for k in range(1, SIDE):
        pl.semaphore_signal(barrier, 1, device_id=(at(twin, k), panel), device_id_type=MESH)
    mates = [at(dz, k) for k in far for dz in (twin, 0)] + [at(twin, 0)]
    for k in range(1, panels):
        pl.semaphore_signal(
            barrier, 1, device_id=(me, lax.rem(panel + k, panels)), device_id_type=MESH
        )

    load_x.wait()
    load_order.wait()
    x4 = jnp.concatenate([x_ref[...]] * 4, axis=0)
    point = iota((LANES, points), 1)
    hots = []
    for b in range(points // LANES):
        row = jnp.broadcast_to(order_ref[b : b + 1, :], (LANES, LANES))
        col = jnp.concatenate([row.T] * (points // LANES), axis=1)
        hots.append((col == point).astype(F32).astype(BF16))
    sorted_ref[pl.ds(0, points), :] = dot_t(jnp.concatenate(hots, axis=0), x4)
    sorted_ref[pl.ds(points, CAP), :] = jnp.zeros((CAP, LANES), F32)

    load_counts.wait()
    part = iota((8, LANES), 1) // channels

    def fill(m, start):
        cuts = [sorted_ref[pl.ds(start + 8 * q, 8), :] for q in range(4)]
        low = jnp.where(part == 0, cuts[0], cuts[1])
        high = jnp.where(part == 2, cuts[2], cuts[3])
        dy = lax.rem(m, SIDE)
        dz = lax.rem(m // SIDE + (y + dy) // SIDE, rows)
        out[dz, dy] = jnp.where(part < 2, low, high).astype(BF16)
        return start + counts_ref[m]

    lax.fori_loop(0, devices, fill, 0, unroll=8)

    load_local.wait()
    load_cross.wait()
    tiles = local_v.shape[2]
    lane = iota((tiles, LANES), 1)
    leaf = lane % leaves
    want = jnp.where(
        lane < leaves, leaf,
        jnp.where(
            lane < 2 * leaves, 16 + leaf // 2,
            jnp.where(lane < 3 * leaves, 24 + leaf // 4, 28 + leaf // 8),
        ),
    )
    pick_local = ((iota((tiles, LANES), 0) == want) & (lane < 4 * leaves)).astype(F32).astype(BF16)
    tiles_x = cross_v.shape[2]
    lane = iota((tiles_x, LANES), 1)
    level = lane // leaves - 4
    firsts = [2 * devices - 2 * devices // 2**t + me // 2**t for t in range(CROSS)]
    want = jnp.where(
        level == 0, firsts[0],
        jnp.where(level == 1, firsts[1], jnp.where(level == 2, firsts[2], firsts[3])),
    )
    pick_cross = ((iota((tiles_x, LANES), 0) == want) & (level >= 0)).astype(F32).astype(BF16)
    chain = jnp.zeros((RANK * RANK, LANES), F32)
    for source, pick in ((local_v, pick_local), (cross_v, pick_cross)):
        flat = source[...].reshape(RANK * RANK, source.shape[2])
        for term in split3(flat):
            chain = chain + dot(term, pick)
    for step in (leaves, 2 * leaves, 4 * leaves):
        left = chain.reshape(RANK, RANK, LANES)
        right = pltpu.roll(chain, LANES - step, 1).reshape(RANK, RANK, LANES)
        total = left[:, 0:1, :] * right[0:1]
        for k in range(1, RANK):
            total = total + left[:, k : k + 1, :] * right[k : k + 1]
        chain = total.reshape(RANK * RANK, LANES)
    hi, mid, low = split3(chain)
    lane = iota((RANK * RANK, LANES), 1)
    terms = jnp.where(
        lane < leaves, hi.astype(F32),
        jnp.where(
            lane < 2 * leaves, pltpu.roll(mid.astype(F32), leaves, 1),
            jnp.where(lane < 3 * leaves, pltpu.roll(low.astype(F32), 2 * leaves, 1), 0.0),
        ),
    ).astype(BF16)
    spread = iota((LANES, points), 0)
    spread = ((spread % leaves == iota((LANES, points), 1) // LEAF) & (spread < 3 * leaves))
    path = dot(terms, spread.astype(F32).astype(BF16)).reshape(RANK, RANK, points)
    load_bases.wait()
    bases = bases_ref[...].astype(F32)
    weights = path[0] * bases[0:1]
    for k in range(1, RANK):
        weights = weights + path[k] * bases[k : k + 1]
    parts = split3(weights)
    weights3 = jnp.concatenate(parts, axis=0)

    pl.semaphore_wait(barrier, 2 * (SIDE - 1) + rows - 1 + panels - 1)

    one = [
        pltpu.make_async_remote_copy(
            out.at[k], middle.at[k], one_send, one_recv,
            device_id=(at(k, 0), panel), device_id_type=MESH,
        )
        for k in far
    ]
    for copy in one:
        copy.start()
    middle[0] = out[0]
    load_countv.wait()
    counts = countv_ref[...].astype(F32)
    square = (devices, devices)
    upto = (iota(square, 0) <= iota(square, 1)).astype(F32).astype(BF16)
    ends = dot(jnp.broadcast_to(counts, (8, devices)).astype(BF16), upto)[0:1]
    diagonal = jnp.where(iota(square, 0) == iota(square, 1), jnp.broadcast_to(counts, square), 0.0)
    counts_col = dot(diagonal.astype(BF16), jnp.ones((devices, LANES), BF16))
    both = jnp.concatenate([counts_col, jnp.ones((devices, LANES), F32)], axis=1).astype(BF16)
    position = iota((points, devices), 0).astype(F32)
    passed = dot((ends <= position).astype(F32).astype(BF16), both)
    within = (iota((points, LANES), 0).astype(F32) - passed[:, :LANES]).astype(jnp.int32)
    run = passed[:, LANES:].astype(jnp.int32)
    dy = run % SIDE
    dz = (run // SIDE + (dy > y).astype(jnp.int32)) % rows
    slot = (dy * rows + dz) * 8 + within % 8
    slots = devices * 8
    hot_ref[...] = (
        (jnp.concatenate([slot] * (slots // LANES), axis=1) == iota((points, slots), 1))
        .astype(F32)
        .astype(BF16)
    )

    lower = (iota(square, 1) <= iota(square, 0)).astype(F32).astype(BF16)
    ends_col = dot(lower, counts_col.astype(BF16))
    passed_row = (
        (jnp.concatenate([ends_col] * (points // LANES), axis=1) <= iota((devices, points), 1).astype(F32))
        .astype(F32)
        .astype(BF16)
    )
    starts_row = dot(jnp.broadcast_to(counts, (8, devices)).astype(BF16), passed_row)[0:1]
    quarter_row = (iota((1, points), 1).astype(F32) - starts_row).astype(jnp.int32) // 8
    pair = jnp.concatenate([parts[0], parts[1]], axis=0).astype(F32)
    keep = quarter_row == iota((4 * 2 * RANK, points), 0) // (2 * RANK)
    spaced = jnp.where(keep, jnp.concatenate([pair] * 4, axis=0), 0.0).astype(BF16)
    spaced = dot(spaced, hot_ref[...]).T.astype(BF16)
    weight_out[...] = spaced.reshape(SIDE, slots // SIDE, LANES)

    for k in far:
        pltpu.make_async_remote_copy(
            weight_out.at[k], weight_in.at[k], weight_send, weight_recv,
            device_id=(at(0, SIDE - k), panel), device_id_type=MESH,
        ).start()
    weight_in[0] = weight_out[0]

    wide = jnp.concatenate([p for p in parts for _ in range(8)], axis=0)
    gram = dot_t(weights3, wide)
    gram = gram[0:RANK] + gram[RANK : 2 * RANK] + gram[2 * RANK :]
    gram = gram[:, 0:LANES] + gram[:, LANES : 2 * LANES] + gram[:, 2 * LANES :]
    packed = pack2(gram)
    gram_out[...] = packed
    gram_in[rank_in] = packed

    for peer in mates:
        pltpu.make_async_remote_copy(
            gram_out, gram_in.at[rank_in], gram_send, gram_recv,
            device_id=(peer, panel), device_id_type=MESH,
        ).start()

    quarter_ref[...] = (within // 8 == iota((points, LANES), 1) // channels).astype(F32)

    others = pl.ds(1, SIDE - 1)
    pltpu.make_async_copy(weight_in.at[others], weight_in.at[others], weight_recv).wait()
    weights_in = weight_in[...].reshape(slots, LANES).astype(F32).T.astype(BF16)
    pltpu.make_async_copy(middle.at[others], middle.at[others], one_recv).wait()

    held = jnp.concatenate(
        [middle[:, k].astype(F32).reshape(rows * 8, LANES) for k in range(SIDE)], axis=0
    ).astype(BF16)
    moment = dot(weights_in, held)
    part = iota((2 * RANK, LANES), 1) // channels
    moment = sum(
        jnp.where(part == q, moment[q * 2 * RANK : (q + 1) * 2 * RANK], 0.0) for q in range(4)
    )
    moment = group_sum(moment[:RANK] + moment[RANK:], channels)
    part = iota((4, LANES), 1) // channels
    low = jnp.where(part == 0, moment[0:4], moment[4:8])
    high = jnp.where(part == 2, moment[8:12], moment[12:16])
    packed = jnp.where(part < 2, low, high)
    moment_out[...] = packed
    moment_in[rank_in] = packed

    for peer in mates:
        pltpu.make_async_remote_copy(
            moment_out, moment_in.at[rank_in], moment_send, moment_recv,
            device_id=(peer, panel), device_id_type=MESH,
        ).start()

    two = [
        pltpu.make_async_remote_copy(
            middle.at[:, k], recv.at[k], two_send, two_recv,
            device_id=(at(0, k), panel), device_id_type=MESH,
        )
        for k in far
    ]
    for copy in two:
        copy.start()
    recv[0] = middle[:, 0]

    peers = pl.ds(0, group - 1)
    pltpu.make_async_copy(gram_in.at[peers], gram_in.at[peers], gram_recv).wait()
    sub = iota((RANK, LANES), 0)
    lane = iota((RANK, LANES), 1)
    tableau = jnp.where(
        lane < RANK, unpack2(jnp.sum(gram_in[...], axis=0)), (lane - RANK == sub).astype(F32)
    )
    for k in range(RANK - 1):
        ratio = tableau[:, k : k + 1] / tableau[k : k + 1, k : k + 1]
        tableau = tableau - jnp.where(sub > k, ratio * tableau[k : k + 1, :], 0.0)
    pivots = jnp.sum(jnp.where(lane == sub, tableau, 0.0), axis=1, keepdims=True)
    tableau = tableau * (1.0 / jnp.sqrt(pivots))
    factor_ref[0] = jnp.where(lane >= sub, tableau, 0.0)[:, :RANK]
    inverse = tableau[:, RANK : 2 * RANK]

    pltpu.make_async_copy(moment_in.at[peers], moment_in.at[peers], moment_recv).wait()
    packed = jnp.sum(moment_in[...], axis=0)
    moment = jnp.concatenate(
        [packed[:, q * channels : (q + 1) * channels] for q in range(4)], axis=0
    )
    coeffs = dot(inverse, moment, HIGH)
    coeffs_ref[0] = coeffs
    packed = pack2(dot_t(coeffs, jnp.concatenate([coeffs] * 8, axis=0), HIGH))
    top_out[...] = packed
    top_in[panel] = packed

    def send_top(m, carry):
        pltpu.make_async_remote_copy(
            top_out, top_in.at[panel], top_send, top_recv,
            device_id=(me, lax.rem(panel + m, panels)), device_id_type=MESH,
        ).start()
        return carry

    lax.fori_loop(1, panels, send_top, 0, unroll=7)

    pltpu.make_async_copy(recv.at[others], recv.at[others], two_recv).wait()

    received = recv[...].astype(F32).reshape(slots, LANES).astype(BF16)
    relaid = dot(hot_ref[...], received)
    relaid = jnp.where(quarter_ref[...] > 0.5, relaid, 0.0).astype(BF16)

    fold = (iota((channels, LANES), 1) % channels == iota((channels, LANES), 0)).astype(F32).astype(BF16)
    for n in range(leaves):
        columns = dot_t(fold, relaid[n * LEAF : (n + 1) * LEAF]).astype(BF16)
        own[n] = columns
        ext[n + REACH] = columns
    right = lax.rem(me + 1, devices)
    left = lax.rem(me + devices - 1, devices)
    to_left = pltpu.make_async_remote_copy(
        own.at[pl.ds(0, REACH)], ext.at[pl.ds(leaves + REACH, REACH)], left_send, left_recv,
        device_id=(left, panel), device_id_type=MESH,
    )
    to_right = pltpu.make_async_remote_copy(
        own.at[pl.ds(leaves - REACH, REACH)], ext.at[pl.ds(0, REACH)], right_send, right_recv,
        device_id=(right, panel), device_id_type=MESH,
    )
    has_left = me > 0
    has_right = me < devices - 1

    @pl.when(has_left)
    def _():
        to_left.start()

    @pl.when(has_right)
    def _():
        to_right.start()

    @pl.when(me == 0)
    def _():
        ext[pl.ds(0, REACH)] = jnp.zeros((REACH, channels, LEAF), BF16)

    @pl.when(me == devices - 1)
    def _():
        ext[pl.ds(leaves + REACH, REACH)] = jnp.zeros((REACH, channels, LEAF), BF16)


    load_cols.wait()
    load_scales.wait()
    load_mats.wait()

    def near_leaf(i, source, first):
        rows = jnp.concatenate(
            [source[jnp.clip(cols_ref[NEAR * i + t] - first, 0, source.shape[0] - 1)] for t in range(NEAR)],
            axis=0,
        )
        width = NEAR * LEAF
        prod = dot(rows, mats[:, i * width : (i + 1) * width])
        lower = iota((channels, LANES), 1) < LEAF
        halves = []
        for h in range(2):
            cut = prod[:, h * LANES : (h + 1) * LANES]
            halves.append(
                jnp.where(
                    lower,
                    cut[2 * h * channels : (2 * h + 1) * channels] * scales_ref[NEAR * i + 2 * h],
                    cut[(2 * h + 1) * channels : (2 * h + 2) * channels] * scales_ref[NEAR * i + 2 * h + 1],
                )
            )
        both = halves[0] + halves[1]
        return both + pltpu.roll(both, LEAF, 1)

    def near_pair(i, source, first):
        a = near_leaf(i, source, first)
        b = near_leaf(i + 1, source, first)
        lower = iota((channels, LANES), 1) < LEAF
        near_ref[:, i * LEAF : (i + 2) * LEAF] = jnp.where(lower, a, b).astype(BF16)

    for i in range(REACH, leaves - REACH, 2):
        near_pair(i, own, me * leaves)

    @pl.when(has_right)
    def _():
        to_left.wait_recv()

    @pl.when(has_left)
    def _():
        to_right.wait_recv()

    first = me * leaves - REACH
    near_pair(0, ext, first)
    near_pair(leaves - 2, ext, first)

    peers = pl.ds(0, panels - 1)
    pltpu.make_async_copy(top_in.at[peers], top_in.at[peers], top_recv).wait()
    topgram_ref[0] = unpack2(jnp.sum(top_in[...], axis=0))[:, :RANK]

    pltpu.make_async_copy(out.at[others], out.at[others], one_send).wait()
    pltpu.make_async_copy(weight_in.at[others], weight_in.at[others], weight_send).wait()
    pltpu.make_async_copy(recv.at[others], recv.at[others], two_send).wait()
    peers = pl.ds(0, group - 1)
    pltpu.make_async_copy(gram_in.at[peers], gram_in.at[peers], gram_send).wait()
    pltpu.make_async_copy(moment_in.at[peers], moment_in.at[peers], moment_send).wait()
    peers = pl.ds(0, panels - 1)
    pltpu.make_async_copy(top_in.at[peers], top_in.at[peers], top_send).wait()
    @pl.when(has_left)
    def _():
        to_left.wait_send()

    @pl.when(has_right)
    def _():
        to_right.wait_send()


def on_device(
    inputs, local_order, run_counts, near_cols, near_blocks, near_scales, leaf_bases, local_tiles,
    cross_tiles,
):
    devices = lax.axis_size("cluster")
    panels = lax.axis_size("panel")
    channels, points = inputs.shape
    leaves = points // LEAF
    group = 2**CROSS
    vmem = pl.BlockSpec(memory_space=pltpu.VMEM)
    hbm = pl.BlockSpec(memory_space=pl.ANY)
    dma = pltpu.SemaphoreType.DMA
    operands = (
        inputs,
        local_order.reshape(points // LANES, LANES),
        run_counts,
        run_counts.reshape(1, devices),
        near_cols,
        near_scales,
        near_blocks,
        leaf_bases,
        jnp.transpose(local_tiles, (1, 2, 0)),
        jnp.transpose(cross_tiles, (1, 2, 0)),
    )
    operands = [pltpu.with_memory_space_constraint(x, pltpu.HBM) for x in operands]
    spaces = [pltpu.VMEM, pltpu.VMEM, pltpu.SMEM, pltpu.VMEM, pltpu.SMEM, pltpu.SMEM] + [pltpu.VMEM] * 4
    slots = (SIDE, SIDE, 8, LANES)
    shapes = (
        ((channels, points), BF16),
        ((1, RANK, channels), F32),
        ((1, RANK, RANK), F32),
        ((1, RANK, RANK), F32),
    )
    results = pl.pallas_call(
        functools.partial(body, devices, panels),
        out_shape=tuple(pltpu.VMEM(*s) for s in shapes),
        in_specs=[hbm] * len(operands),
        out_specs=(vmem,) * 4,
        scratch_shapes=[space(x.shape, x.dtype) for space, x in zip(spaces, operands)]
        + [
            pltpu.VMEM((points + CAP, LANES), F32),
            pltpu.VMEM(slots, BF16),
            pltpu.VMEM(slots, BF16),
            pltpu.VMEM(slots, BF16),
            pltpu.VMEM((SIDE, devices * 8 // SIDE, LANES), BF16),
            pltpu.VMEM((SIDE, devices * 8 // SIDE, LANES), BF16),
            pltpu.VMEM((leaves, channels, LEAF), BF16),
            pltpu.VMEM((leaves + 2 * REACH, channels, LEAF), BF16),
            pltpu.VMEM((4, LANES), F32),
            pltpu.VMEM((group, 4, LANES), F32),
            pltpu.VMEM((2, LANES), F32),
            pltpu.VMEM((group, 2, LANES), F32),
            pltpu.VMEM((2, LANES), F32),
            pltpu.VMEM((panels, 2, LANES), F32),
            pltpu.VMEM((points, devices * 8), BF16),
            pltpu.VMEM((points, LANES), F32),
            dma((len(operands),)),
        ]
        + [dma] * 16,
        compiler_params=pltpu.CompilerParams(
            collective_id=0, has_side_effects=True, vmem_limit_bytes=48 * 2**20
        ),
    )(*operands)
    return pl.pallas_call(
        store,
        out_shape=tuple(jax.ShapeDtypeStruct(*s) for s in shapes),
        in_specs=[hbm] * 4,
        out_specs=(hbm,) * 4,
        scratch_shapes=[dma((4,))],
    )(*[pltpu.with_memory_space_constraint(x, pltpu.VMEM) for x in results])


def store(*refs):
    sems = refs[8]
    copies = [pltpu.make_async_copy(refs[k], refs[4 + k], sems.at[k]) for k in range(4)]
    for copy in copies:
        copy.start()
    for copy in copies:
        copy.wait()


def solution(mesh):
    placed = (
        P("panel", "cluster"),
        P("cluster"),
        P(),
        P("cluster"),
        P(None, "cluster"),
        P("cluster"),
        P(None, "cluster"),
        P("cluster", None, None),
        P(),
    )
    return jax.shard_map(
        on_device,
        mesh=mesh,
        in_specs=placed,
        out_specs=(
            P("panel", "cluster"),
            P("cluster", None, "panel"),
            P("cluster", None, None),
            P("cluster", None, None),
        ),
        check_vma=False,
    )
```

```python
import functools

import jax
import jax.numpy as jnp
from jax import lax
from jax.experimental import pallas as pl
from jax.experimental.pallas import tpu as pltpu
from jax.sharding import PartitionSpec as P

LEAF = 64
RANK = 16
NEAR = 4
REACH = 2
CROSS = 4
CAP = 32
SIDE = 8
LANES = 128
MESH = pl.DeviceIdType.MESH
HIGH = lax.Precision.HIGHEST
F32 = jnp.float32
BF16 = jnp.bfloat16


def iota(shape, dim):
    return lax.broadcasted_iota(jnp.int32, shape, dim)


def dot(a, b, precision=None):
    return lax.dot_general(
        a, b, (((1,), (0,)), ((), ())), precision=precision, preferred_element_type=F32
    )


def dot_t(a, b, precision=None):
    return lax.dot_general(
        a, b, (((1,), (1,)), ((), ())), precision=precision, preferred_element_type=F32
    )


def split3(x):
    hi = x.astype(BF16)
    rest = x - hi.astype(F32)
    mid = rest.astype(BF16)
    low = (rest - mid.astype(F32)).astype(BF16)
    return hi, mid, low


def group_sum(x, width):
    shift = LANES // 2
    while shift >= width:
        x = x + pltpu.roll(x, shift, 1)
        shift //= 2
    return x


def pack2(x):
    keep = iota((RANK, LANES), 0) % 8 == iota((RANK, LANES), 1) // RANK
    return jnp.where(keep, x, 0.0).reshape(2, 8, LANES).sum(axis=1)


def unpack2(x):
    rows = jnp.concatenate(
        [jnp.broadcast_to(x[0:1], (8, LANES)), jnp.broadcast_to(x[1:2], (8, LANES))], axis=0
    )
    keep = iota((RANK, LANES), 0) % 8 == iota((RANK, LANES), 1) // RANK
    return group_sum(jnp.where(keep, rows, 0.0), RANK)


def body(
    devices, panels, x_hbm, order_hbm, counts_hbm, countv_hbm, cols_hbm, scales_hbm, mats_hbm,
    bases_hbm, local_hbm, cross_hbm, near_ref, coeffs_ref, factor_ref, topgram_ref,
    x_ref, order_ref, counts_ref, countv_ref, cols_ref, scales_ref, mats, bases_ref, local_v, cross_v,
    sorted_ref, out, middle, recv, weight_out, weight_in, own, ext, moment_out, moment_in, gram_out, gram_in,
    top_out, top_in, hot_ref, quarter_ref,
    load_sems, one_send, one_recv, weight_send, weight_recv, two_send, two_recv, gram_send, gram_recv, moment_send, moment_recv,
    top_send, top_recv, left_send, left_recv, right_send, right_recv,
):
    me = lax.axis_index("cluster")
    panel = lax.axis_index("panel")
    group = 2**CROSS
    rank_in = lax.rem(me, group)
    channels, points = x_ref.shape
    leaves = points // LEAF

    rows = devices // SIDE
    y = lax.rem(me, SIDE)
    z = me // SIDE

    def load(source, target, at):
        copy = pltpu.make_async_copy(source, target, load_sems.at[at])
        copy.start()
        return copy

    load_x = load(x_hbm, x_ref, 0)
    load_order = load(order_hbm, order_ref, 1)
    load_counts = load(counts_hbm, counts_ref, 2)
    load_local = load(local_hbm, local_v, 3)
    load_cross = load(cross_hbm, cross_v, 4)
    load_bases = load(bases_hbm, bases_ref, 5)
    load_countv = load(countv_hbm, countv_ref, 6)
    load_cols = load(cols_hbm, cols_ref, 7)
    load_scales = load(scales_hbm, scales_ref, 8)
    load_mats = load(mats_hbm, mats, 9)

    barrier = pltpu.get_barrier_semaphore()

    def at(dz, dy):
        return lax.rem(z + dz, rows) * SIDE + lax.rem(y + dy, SIDE)

    far = sorted(range(1, SIDE), key=lambda k: -min(k, SIDE - k))
    for k in far:
        pl.semaphore_signal(barrier, 1, device_id=(at(k, 0), panel), device_id_type=MESH)
    for k in far:
        pl.semaphore_signal(barrier, 1, device_id=(at(0, k), panel), device_id_type=MESH)
    twin = 1 - 2 * lax.rem(z, 2) + rows
    for k in range(1, SIDE):
        pl.semaphore_signal(barrier, 1, device_id=(at(twin, k), panel), device_id_type=MESH)
    mates = [at(dz, k) for k in far for dz in (twin, 0)] + [at(twin, 0)]
    for k in range(1, panels):
        pl.semaphore_signal(
            barrier, 1, device_id=(me, lax.rem(panel + k, panels)), device_id_type=MESH
        )

    load_x.wait()
    load_order.wait()
    x4 = jnp.concatenate([x_ref[...]] * 4, axis=0)
    point = iota((LANES, points), 1)
    hots = []
    for b in range(points // LANES):
        row = jnp.broadcast_to(order_ref[b : b + 1, :], (LANES, LANES))
        col = jnp.concatenate([row.T] * (points // LANES), axis=1)
        hots.append((col == point).astype(F32).astype(BF16))
    sorted_ref[pl.ds(0, points), :] = dot_t(jnp.concatenate(hots, axis=0), x4)
    sorted_ref[pl.ds(points, CAP), :] = jnp.zeros((CAP, LANES), F32)

    load_counts.wait()
    part = iota((8, LANES), 1) // channels

    def fill(m, start):
        cuts = [sorted_ref[pl.ds(start + 8 * q, 8), :] for q in range(4)]
        low = jnp.where(part == 0, cuts[0], cuts[1])
        high = jnp.where(part == 2, cuts[2], cuts[3])
        dy = lax.rem(m, SIDE)
        dz = lax.rem(m // SIDE + (y + dy) // SIDE, rows)
        out[dz, dy] = jnp.where(part < 2, low, high).astype(BF16)
        return start + counts_ref[m]

    lax.fori_loop(0, devices, fill, 0, unroll=8)

    load_local.wait()
    load_cross.wait()
    tiles = local_v.shape[2]
    lane = iota((tiles, LANES), 1)
    leaf = lane % leaves
    want = jnp.where(
        lane < leaves, leaf,
        jnp.where(
            lane < 2 * leaves, 16 + leaf // 2,
            jnp.where(lane < 3 * leaves, 24 + leaf // 4, 28 + leaf // 8),
        ),
    )
    pick_local = ((iota((tiles, LANES), 0) == want) & (lane < 4 * leaves)).astype(F32).astype(BF16)
    tiles_x = cross_v.shape[2]
    lane = iota((tiles_x, LANES), 1)
    level = lane // leaves - 4
    firsts = [2 * devices - 2 * devices // 2**t + me // 2**t for t in range(CROSS)]
    want = jnp.where(
        level == 0, firsts[0],
        jnp.where(level == 1, firsts[1], jnp.where(level == 2, firsts[2], firsts[3])),
    )
    pick_cross = ((iota((tiles_x, LANES), 0) == want) & (level >= 0)).astype(F32).astype(BF16)
    chain = jnp.zeros((RANK * RANK, LANES), F32)
    for source, pick in ((local_v, pick_local), (cross_v, pick_cross)):
        flat = source[...].reshape(RANK * RANK, source.shape[2])
        for term in split3(flat):
            chain = chain + dot(term, pick)
    for step in (leaves, 2 * leaves, 4 * leaves):
        left = chain.reshape(RANK, RANK, LANES)
        right = pltpu.roll(chain, LANES - step, 1).reshape(RANK, RANK, LANES)
        total = left[:, 0:1, :] * right[0:1]
        for k in range(1, RANK):
            total = total + left[:, k : k + 1, :] * right[k : k + 1]
        chain = total.reshape(RANK * RANK, LANES)
    hi, mid, low = split3(chain)
    lane = iota((RANK * RANK, LANES), 1)
    terms = jnp.where(
        lane < leaves, hi.astype(F32),
        jnp.where(
            lane < 2 * leaves, pltpu.roll(mid.astype(F32), leaves, 1),
            jnp.where(lane < 3 * leaves, pltpu.roll(low.astype(F32), 2 * leaves, 1), 0.0),
        ),
    ).astype(BF16)
    spread = iota((LANES, points), 0)
    spread = ((spread % leaves == iota((LANES, points), 1) // LEAF) & (spread < 3 * leaves))
    path = dot(terms, spread.astype(F32).astype(BF16)).reshape(RANK, RANK, points)
    load_bases.wait()
    bases = bases_ref[...].astype(F32)
    weights = path[0] * bases[0:1]
    for k in range(1, RANK):
        weights = weights + path[k] * bases[k : k + 1]
    parts = split3(weights)
    weights3 = jnp.concatenate(parts, axis=0)

    pl.semaphore_wait(barrier, 2 * (SIDE - 1) + rows - 1 + panels - 1)

    one = [
        pltpu.make_async_remote_copy(
            out.at[k], middle.at[k], one_send, one_recv,
            device_id=(at(k, 0), panel), device_id_type=MESH,
        )
        for k in far
    ]
    for copy in one:
        copy.start()
    middle[0] = out[0]
    load_countv.wait()
    counts = countv_ref[...].astype(F32)
    square = (devices, devices)
    upto = (iota(square, 0) <= iota(square, 1)).astype(F32).astype(BF16)
    ends = dot(jnp.broadcast_to(counts, (8, devices)).astype(BF16), upto)[0:1]
    diagonal = jnp.where(iota(square, 0) == iota(square, 1), jnp.broadcast_to(counts, square), 0.0)
    counts_col = dot(diagonal.astype(BF16), jnp.ones((devices, LANES), BF16))
    both = jnp.concatenate([counts_col, jnp.ones((devices, LANES), F32)], axis=1).astype(BF16)
    position = iota((points, devices), 0).astype(F32)
    passed = dot((ends <= position).astype(F32).astype(BF16), both)
    within = (iota((points, LANES), 0).astype(F32) - passed[:, :LANES]).astype(jnp.int32)
    run = passed[:, LANES:].astype(jnp.int32)
    dy = run % SIDE
    dz = (run // SIDE + (dy > y).astype(jnp.int32)) % rows
    slot = (dy * rows + dz) * 8 + within % 8
    slots = devices * 8
    hot_ref[...] = (
        (jnp.concatenate([slot] * (slots // LANES), axis=1) == iota((points, slots), 1))
        .astype(F32)
        .astype(BF16)
    )

    lower = (iota(square, 1) <= iota(square, 0)).astype(F32).astype(BF16)
    ends_col = dot(lower, counts_col.astype(BF16))
    passed_row = (
        (jnp.concatenate([ends_col] * (points // LANES), axis=1) <= iota((devices, points), 1).astype(F32))
        .astype(F32)
        .astype(BF16)
    )
    starts_row = dot(jnp.broadcast_to(counts, (8, devices)).astype(BF16), passed_row)[0:1]
    quarter_row = (iota((1, points), 1).astype(F32) - starts_row).astype(jnp.int32) // 8
    pair = jnp.concatenate([parts[0], parts[1]], axis=0).astype(F32)
    keep = quarter_row == iota((4 * 2 * RANK, points), 0) // (2 * RANK)
    spaced = jnp.where(keep, jnp.concatenate([pair] * 4, axis=0), 0.0).astype(BF16)
    spaced = dot(spaced, hot_ref[...]).T.astype(BF16)
    weight_out[...] = spaced.reshape(SIDE, slots // SIDE, LANES)

    for k in far:
        pltpu.make_async_remote_copy(
            weight_out.at[k], weight_in.at[k], weight_send, weight_recv,
            device_id=(at(0, SIDE - k), panel), device_id_type=MESH,
        ).start()
    weight_in[0] = weight_out[0]

    wide = jnp.concatenate([p for p in parts for _ in range(8)], axis=0)
    gram = dot_t(weights3, wide)
    gram = gram[0:RANK] + gram[RANK : 2 * RANK] + gram[2 * RANK :]
    gram = gram[:, 0:LANES] + gram[:, LANES : 2 * LANES] + gram[:, 2 * LANES :]
    packed = pack2(gram)
    gram_out[...] = packed
    gram_in[rank_in] = packed

    for peer in mates:
        pltpu.make_async_remote_copy(
            gram_out, gram_in.at[rank_in], gram_send, gram_recv,
            device_id=(peer, panel), device_id_type=MESH,
        ).start()

    quarter_ref[...] = (within // 8 == iota((points, LANES), 1) // channels).astype(F32)

    others = pl.ds(1, SIDE - 1)
    pltpu.make_async_copy(weight_in.at[others], weight_in.at[others], weight_recv).wait()
    weights_in = weight_in[...].reshape(slots, LANES).astype(F32).T.astype(BF16)
    pltpu.make_async_copy(middle.at[others], middle.at[others], one_recv).wait()

    held = jnp.concatenate(
        [middle[:, k].astype(F32).reshape(rows * 8, LANES) for k in range(SIDE)], axis=0
    ).astype(BF16)
    moment = dot(weights_in, held)
    part = iota((2 * RANK, LANES), 1) // channels
    moment = sum(
        jnp.where(part == q, moment[q * 2 * RANK : (q + 1) * 2 * RANK], 0.0) for q in range(4)
    )
    moment = group_sum(moment[:RANK] + moment[RANK:], channels)
    part = iota((4, LANES), 1) // channels
    low = jnp.where(part == 0, moment[0:4], moment[4:8])
    high = jnp.where(part == 2, moment[8:12], moment[12:16])
    packed = jnp.where(part < 2, low, high)
    moment_out[...] = packed
    moment_in[rank_in] = packed

    for peer in mates:
        pltpu.make_async_remote_copy(
            moment_out, moment_in.at[rank_in], moment_send, moment_recv,
            device_id=(peer, panel), device_id_type=MESH,
        ).start()

    peers = pl.ds(0, group - 1)
    pltpu.make_async_copy(gram_in.at[peers], gram_in.at[peers], gram_recv).wait()
    sub = iota((RANK, LANES), 0)
    lane = iota((RANK, LANES), 1)
    tableau = jnp.where(
        lane < RANK, unpack2(jnp.sum(gram_in[...], axis=0)), (lane - RANK == sub).astype(F32)
    )
    for k in range(RANK - 1):
        ratio = tableau[:, k : k + 1] / tableau[k : k + 1, k : k + 1]
        tableau = tableau - jnp.where(sub > k, ratio * tableau[k : k + 1, :], 0.0)
    pivots = jnp.sum(jnp.where(lane == sub, tableau, 0.0), axis=1, keepdims=True)
    tableau = tableau * (1.0 / jnp.sqrt(pivots))
    factor_ref[0] = jnp.where(lane >= sub, tableau, 0.0)[:, :RANK]
    inverse = tableau[:, RANK : 2 * RANK]

    two = [
        pltpu.make_async_remote_copy(
            middle.at[:, k], recv.at[k], two_send, two_recv,
            device_id=(at(0, k), panel), device_id_type=MESH,
        )
        for k in far
    ]
    for copy in two:
        copy.start()
    recv[0] = middle[:, 0]

    pltpu.make_async_copy(moment_in.at[peers], moment_in.at[peers], moment_recv).wait()
    packed = jnp.sum(moment_in[...], axis=0)
    moment = jnp.concatenate(
        [packed[:, q * channels : (q + 1) * channels] for q in range(4)], axis=0
    )
    coeffs = dot(inverse, moment, HIGH)
    coeffs_ref[0] = coeffs
    terms = split3(coeffs)
    gram = dot_t(
        jnp.concatenate(terms, axis=0),
        jnp.concatenate([p for p in terms for _ in range(8)], axis=0),
    )
    gram = gram[0:RANK] + gram[RANK : 2 * RANK] + gram[2 * RANK :]
    packed = pack2(gram[:, 0:LANES] + gram[:, LANES : 2 * LANES] + gram[:, 2 * LANES :])
    top_out[...] = packed
    top_in[panel] = packed

    for k in sorted(range(1, panels), key=lambda k: -min(k, panels - k)):
        pltpu.make_async_remote_copy(
            top_out, top_in.at[panel], top_send, top_recv,
            device_id=(me, lax.rem(panel + k, panels)), device_id_type=MESH,
        ).start()

    pltpu.make_async_copy(recv.at[others], recv.at[others], two_recv).wait()

    received = recv[...].astype(F32).reshape(slots, LANES).astype(BF16)
    relaid = dot(hot_ref[...], received)
    relaid = jnp.where(quarter_ref[...] > 0.5, relaid, 0.0).astype(BF16)

    fold = (iota((channels, LANES), 1) % channels == iota((channels, LANES), 0)).astype(F32).astype(BF16)
    for n in range(leaves):
        columns = dot_t(fold, relaid[n * LEAF : (n + 1) * LEAF]).astype(BF16)
        own[n] = columns
        ext[n + REACH] = columns
    right = lax.rem(me + 1, devices)
    left = lax.rem(me + devices - 1, devices)
    to_left = pltpu.make_async_remote_copy(
        own.at[pl.ds(0, REACH)], ext.at[pl.ds(leaves + REACH, REACH)], left_send, left_recv,
        device_id=(left, panel), device_id_type=MESH,
    )
    to_right = pltpu.make_async_remote_copy(
        own.at[pl.ds(leaves - REACH, REACH)], ext.at[pl.ds(0, REACH)], right_send, right_recv,
        device_id=(right, panel), device_id_type=MESH,
    )
    has_left = me > 0
    has_right = me < devices - 1

    @pl.when(has_left)
    def _():
        to_left.start()

    @pl.when(has_right)
    def _():
        to_right.start()

    @pl.when(me == 0)
    def _():
        ext[pl.ds(0, REACH)] = jnp.zeros((REACH, channels, LEAF), BF16)

    @pl.when(me == devices - 1)
    def _():
        ext[pl.ds(leaves + REACH, REACH)] = jnp.zeros((REACH, channels, LEAF), BF16)


    load_cols.wait()
    load_scales.wait()
    load_mats.wait()

    def near_leaf(i, source, first):
        rows = jnp.concatenate(
            [source[jnp.clip(cols_ref[NEAR * i + t] - first, 0, source.shape[0] - 1)] for t in range(NEAR)],
            axis=0,
        )
        width = NEAR * LEAF
        prod = dot(rows, mats[:, i * width : (i + 1) * width])
        lower = iota((channels, LANES), 1) < LEAF
        halves = []
        for h in range(2):
            cut = prod[:, h * LANES : (h + 1) * LANES]
            halves.append(
                jnp.where(
                    lower,
                    cut[2 * h * channels : (2 * h + 1) * channels] * scales_ref[NEAR * i + 2 * h],
                    cut[(2 * h + 1) * channels : (2 * h + 2) * channels] * scales_ref[NEAR * i + 2 * h + 1],
                )
            )
        both = halves[0] + halves[1]
        return both + pltpu.roll(both, LEAF, 1)

    def near_pair(i, source, first):
        a = near_leaf(i, source, first)
        b = near_leaf(i + 1, source, first)
        lower = iota((channels, LANES), 1) < LEAF
        near_ref[:, i * LEAF : (i + 2) * LEAF] = jnp.where(lower, a, b).astype(BF16)

    for i in range(REACH, leaves - REACH, 2):
        near_pair(i, own, me * leaves)

    @pl.when(has_right)
    def _():
        to_left.wait_recv()

    @pl.when(has_left)
    def _():
        to_right.wait_recv()

    first = me * leaves - REACH
    near_pair(0, ext, first)
    near_pair(leaves - 2, ext, first)

    peers = pl.ds(0, panels - 1)
    pltpu.make_async_copy(top_in.at[peers], top_in.at[peers], top_recv).wait()
    topgram_ref[0] = unpack2(jnp.sum(top_in[...], axis=0))[:, :RANK]

    pltpu.make_async_copy(out.at[others], out.at[others], one_send).wait()
    pltpu.make_async_copy(weight_in.at[others], weight_in.at[others], weight_send).wait()
    pltpu.make_async_copy(recv.at[others], recv.at[others], two_send).wait()
    peers = pl.ds(0, group - 1)
    pltpu.make_async_copy(gram_in.at[peers], gram_in.at[peers], gram_send).wait()
    pltpu.make_async_copy(moment_in.at[peers], moment_in.at[peers], moment_send).wait()
    peers = pl.ds(0, panels - 1)
    pltpu.make_async_copy(top_in.at[peers], top_in.at[peers], top_send).wait()
    @pl.when(has_left)
    def _():
        to_left.wait_send()

    @pl.when(has_right)
    def _():
        to_right.wait_send()


def on_device(
    inputs, local_order, run_counts, near_cols, near_blocks, near_scales, leaf_bases, local_tiles,
    cross_tiles,
):
    devices = lax.axis_size("cluster")
    panels = lax.axis_size("panel")
    channels, points = inputs.shape
    leaves = points // LEAF
    group = 2**CROSS
    vmem = pl.BlockSpec(memory_space=pltpu.VMEM)
    hbm = pl.BlockSpec(memory_space=pl.ANY)
    dma = pltpu.SemaphoreType.DMA
    operands = (
        inputs,
        local_order.reshape(points // LANES, LANES),
        run_counts,
        run_counts.reshape(1, devices),
        near_cols,
        near_scales,
        near_blocks,
        leaf_bases,
        jnp.transpose(local_tiles, (1, 2, 0)),
        jnp.transpose(cross_tiles, (1, 2, 0)),
    )
    operands = [pltpu.with_memory_space_constraint(x, pltpu.HBM) for x in operands]
    spaces = [pltpu.VMEM, pltpu.VMEM, pltpu.SMEM, pltpu.VMEM, pltpu.SMEM, pltpu.SMEM] + [pltpu.VMEM] * 4
    slots = (SIDE, SIDE, 8, LANES)
    shapes = (
        ((channels, points), BF16),
        ((1, RANK, channels), F32),
        ((1, RANK, RANK), F32),
        ((1, RANK, RANK), F32),
    )
    results = pl.pallas_call(
        functools.partial(body, devices, panels),
        out_shape=tuple(pltpu.VMEM(*s) for s in shapes),
        in_specs=[hbm] * len(operands),
        out_specs=(vmem,) * 4,
        scratch_shapes=[space(x.shape, x.dtype) for space, x in zip(spaces, operands)]
        + [
            pltpu.VMEM((points + CAP, LANES), F32),
            pltpu.VMEM(slots, BF16),
            pltpu.VMEM(slots, BF16),
            pltpu.VMEM(slots, BF16),
            pltpu.VMEM((SIDE, devices * 8 // SIDE, LANES), BF16),
            pltpu.VMEM((SIDE, devices * 8 // SIDE, LANES), BF16),
            pltpu.VMEM((leaves, channels, LEAF), BF16),
            pltpu.VMEM((leaves + 2 * REACH, channels, LEAF), BF16),
            pltpu.VMEM((4, LANES), F32),
            pltpu.VMEM((group, 4, LANES), F32),
            pltpu.VMEM((2, LANES), F32),
            pltpu.VMEM((group, 2, LANES), F32),
            pltpu.VMEM((2, LANES), F32),
            pltpu.VMEM((panels, 2, LANES), F32),
            pltpu.VMEM((points, devices * 8), BF16),
            pltpu.VMEM((points, LANES), F32),
            dma((len(operands),)),
        ]
        + [dma] * 16,
        compiler_params=pltpu.CompilerParams(
            collective_id=0, has_side_effects=True, vmem_limit_bytes=48 * 2**20
        ),
    )(*operands)
    return pl.pallas_call(
        store,
        out_shape=tuple(jax.ShapeDtypeStruct(*s) for s in shapes),
        in_specs=[hbm] * 4,
        out_specs=(hbm,) * 4,
        scratch_shapes=[dma((4,))],
    )(*[pltpu.with_memory_space_constraint(x, pltpu.VMEM) for x in results])


def store(*refs):
    sems = refs[8]
    copies = [pltpu.make_async_copy(refs[k], refs[4 + k], sems.at[k]) for k in range(4)]
    for copy in copies:
        copy.start()
    for copy in copies:
        copy.wait()


def solution(mesh):
    placed = (
        P("panel", "cluster"),
        P("cluster"),
        P(),
        P("cluster"),
        P(None, "cluster"),
        P("cluster"),
        P(None, "cluster"),
        P("cluster", None, None),
        P(),
    )
    return jax.shard_map(
        on_device,
        mesh=mesh,
        in_specs=placed,
        out_specs=(
            P("panel", "cluster"),
            P("cluster", None, "panel"),
            P("cluster", None, None),
            P("cluster", None, None),
        ),
        check_vma=False,
    )
```

```python
import functools

import jax
import jax.numpy as jnp
from jax import lax
from jax.experimental import pallas as pl
from jax.experimental.pallas import tpu as pltpu
from jax.sharding import PartitionSpec as P

LEAF = 64
RANK = 16
NEAR = 4
REACH = 2
CROSS = 4
CAP = 32
SIDE = 8
LANES = 128
MESH = pl.DeviceIdType.MESH
HIGH = lax.Precision.HIGHEST
F32 = jnp.float32
BF16 = jnp.bfloat16


def iota(shape, dim):
    return lax.broadcasted_iota(jnp.int32, shape, dim)


def dot(a, b, precision=None):
    return lax.dot_general(
        a, b, (((1,), (0,)), ((), ())), precision=precision, preferred_element_type=F32
    )


def dot_t(a, b, precision=None):
    return lax.dot_general(
        a, b, (((1,), (1,)), ((), ())), precision=precision, preferred_element_type=F32
    )


def split3(x):
    hi = x.astype(BF16)
    rest = x - hi.astype(F32)
    mid = rest.astype(BF16)
    low = (rest - mid.astype(F32)).astype(BF16)
    return hi, mid, low


def group_sum(x, width):
    shift = LANES // 2
    while shift >= width:
        x = x + pltpu.roll(x, shift, 1)
        shift //= 2
    return x


def pack2(x):
    keep = iota((RANK, LANES), 0) % 8 == iota((RANK, LANES), 1) // RANK
    return jnp.where(keep, x, 0.0).reshape(2, 8, LANES).sum(axis=1)


def unpack2(x):
    rows = jnp.concatenate(
        [jnp.broadcast_to(x[0:1], (8, LANES)), jnp.broadcast_to(x[1:2], (8, LANES))], axis=0
    )
    keep = iota((RANK, LANES), 0) % 8 == iota((RANK, LANES), 1) // RANK
    return group_sum(jnp.where(keep, rows, 0.0), RANK)


def body(
    devices, panels, x_hbm, order_hbm, counts_hbm, countv_hbm, cols_hbm, scales_hbm, mats_hbm,
    bases_hbm, local_hbm, cross_hbm, near_ref, coeffs_ref, factor_ref, topgram_ref,
    x_ref, order_ref, counts_ref, countv_ref, cols_ref, scales_ref, mats, bases_ref, local_v, cross_v,
    sorted_ref, out, middle, recv, weight_out, weight_in, own, ext, moment_out, moment_in, gram_out, gram_in,
    top_out, top_in, hot_ref, quarter_ref,
    load_sems, one_send, one_recv, weight_send, weight_recv, two_send, two_recv, gram_send, gram_recv, moment_send, moment_recv,
    top_send, top_recv, left_send, left_recv, right_send, right_recv,
):
    me = lax.axis_index("cluster")
    panel = lax.axis_index("panel")
    group = 2**CROSS
    rank_in = lax.rem(me, group)
    channels, points = x_ref.shape
    leaves = points // LEAF

    rows = devices // SIDE
    y = lax.rem(me, SIDE)
    z = me // SIDE

    def load(source, target, at):
        copy = pltpu.make_async_copy(source, target, load_sems.at[at])
        copy.start()
        return copy

    load_x = load(x_hbm, x_ref, 0)
    load_order = load(order_hbm, order_ref, 1)
    load_counts = load(counts_hbm, counts_ref, 2)
    load_local = load(local_hbm, local_v, 3)
    load_cross = load(cross_hbm, cross_v, 4)
    load_bases = load(bases_hbm, bases_ref, 5)
    load_countv = load(countv_hbm, countv_ref, 6)
    load_cols = load(cols_hbm, cols_ref, 7)
    load_scales = load(scales_hbm, scales_ref, 8)
    load_mats = load(mats_hbm, mats, 9)

    barrier = pltpu.get_barrier_semaphore()

    def at(dz, dy):
        return lax.rem(z + dz, rows) * SIDE + lax.rem(y + dy, SIDE)

    far = sorted(range(1, SIDE), key=lambda k: -min(k, SIDE - k))
    for k in far:
        pl.semaphore_signal(barrier, 1, device_id=(at(k, 0), panel), device_id_type=MESH)
    for k in far:
        pl.semaphore_signal(barrier, 1, device_id=(at(0, k), panel), device_id_type=MESH)
    twin = 1 - 2 * lax.rem(z, 2) + rows
    for k in range(1, SIDE):
        pl.semaphore_signal(barrier, 1, device_id=(at(twin, k), panel), device_id_type=MESH)
    mates = [at(dz, k) for k in far for dz in (twin, 0)] + [at(twin, 0)]
    for k in range(1, panels):
        pl.semaphore_signal(
            barrier, 1, device_id=(me, lax.rem(panel + k, panels)), device_id_type=MESH
        )

    load_x.wait()
    load_order.wait()
    x4 = jnp.concatenate([x_ref[...]] * 4, axis=0)
    point = iota((LANES, points), 1)
    hots = []
    for b in range(points // LANES):
        row = jnp.broadcast_to(order_ref[b : b + 1, :], (LANES, LANES))
        col = jnp.concatenate([row.T] * (points // LANES), axis=1)
        hots.append((col == point).astype(F32).astype(BF16))
    sorted_ref[pl.ds(0, points), :] = dot_t(jnp.concatenate(hots, axis=0), x4)
    sorted_ref[pl.ds(points, CAP), :] = jnp.zeros((CAP, LANES), F32)

    load_counts.wait()
    part = iota((8, LANES), 1) // channels

    def fill(m, start):
        cuts = [sorted_ref[pl.ds(start + 8 * q, 8), :] for q in range(4)]
        low = jnp.where(part == 0, cuts[0], cuts[1])
        high = jnp.where(part == 2, cuts[2], cuts[3])
        dy = lax.rem(m, SIDE)
        dz = lax.rem(m // SIDE + (y + dy) // SIDE, rows)
        out[dz, dy] = jnp.where(part < 2, low, high).astype(BF16)
        return start + counts_ref[m]

    lax.fori_loop(0, devices, fill, 0, unroll=8)

    load_local.wait()
    load_cross.wait()
    tiles = local_v.shape[2]
    lane = iota((tiles, LANES), 1)
    leaf = lane % leaves
    want = jnp.where(
        lane < leaves, leaf,
        jnp.where(
            lane < 2 * leaves, 16 + leaf // 2,
            jnp.where(lane < 3 * leaves, 24 + leaf // 4, 28 + leaf // 8),
        ),
    )
    pick_local = ((iota((tiles, LANES), 0) == want) & (lane < 4 * leaves)).astype(F32).astype(BF16)
    tiles_x = cross_v.shape[2]
    lane = iota((tiles_x, LANES), 1)
    level = lane // leaves - 4
    firsts = [2 * devices - 2 * devices // 2**t + me // 2**t for t in range(CROSS)]
    want = jnp.where(
        level == 0, firsts[0],
        jnp.where(level == 1, firsts[1], jnp.where(level == 2, firsts[2], firsts[3])),
    )
    pick_cross = ((iota((tiles_x, LANES), 0) == want) & (level >= 0)).astype(F32).astype(BF16)
    chain = jnp.zeros((RANK * RANK, LANES), F32)
    for source, pick in ((local_v, pick_local), (cross_v, pick_cross)):
        flat = source[...].reshape(RANK * RANK, source.shape[2])
        for term in split3(flat):
            chain = chain + dot(term, pick)
    for step in (leaves, 2 * leaves, 4 * leaves):
        left = chain.reshape(RANK, RANK, LANES)
        right = pltpu.roll(chain, LANES - step, 1).reshape(RANK, RANK, LANES)
        total = left[:, 0:1, :] * right[0:1]
        for k in range(1, RANK):
            total = total + left[:, k : k + 1, :] * right[k : k + 1]
        chain = total.reshape(RANK * RANK, LANES)
    hi, mid, low = split3(chain)
    lane = iota((RANK * RANK, LANES), 1)
    terms = jnp.where(
        lane < leaves, hi.astype(F32),
        jnp.where(
            lane < 2 * leaves, pltpu.roll(mid.astype(F32), leaves, 1),
            jnp.where(lane < 3 * leaves, pltpu.roll(low.astype(F32), 2 * leaves, 1), 0.0),
        ),
    ).astype(BF16)
    spread = iota((LANES, points), 0)
    spread = ((spread % leaves == iota((LANES, points), 1) // LEAF) & (spread < 3 * leaves))
    path = dot(terms, spread.astype(F32).astype(BF16)).reshape(RANK, RANK, points)
    load_bases.wait()
    bases = bases_ref[...].astype(F32)
    weights = path[0] * bases[0:1]
    for k in range(1, RANK):
        weights = weights + path[k] * bases[k : k + 1]
    parts = split3(weights)
    weights3 = jnp.concatenate(parts, axis=0)

    pl.semaphore_wait(barrier, 2 * (SIDE - 1) + rows - 1 + panels - 1)

    one = [
        pltpu.make_async_remote_copy(
            out.at[k], middle.at[k], one_send, one_recv,
            device_id=(at(k, 0), panel), device_id_type=MESH,
        )
        for k in far
    ]
    for copy in one:
        copy.start()
    middle[0] = out[0]
    load_countv.wait()
    counts = countv_ref[...].astype(F32)
    square = (devices, devices)
    upto = (iota(square, 0) <= iota(square, 1)).astype(F32).astype(BF16)
    ends = dot(jnp.broadcast_to(counts, (8, devices)).astype(BF16), upto)[0:1]
    diagonal = jnp.where(iota(square, 0) == iota(square, 1), jnp.broadcast_to(counts, square), 0.0)
    counts_col = dot(diagonal.astype(BF16), jnp.ones((devices, LANES), BF16))
    both = jnp.concatenate([counts_col, jnp.ones((devices, LANES), F32)], axis=1).astype(BF16)
    position = iota((points, devices), 0).astype(F32)
    passed = dot((ends <= position).astype(F32).astype(BF16), both)
    within = (iota((points, LANES), 0).astype(F32) - passed[:, :LANES]).astype(jnp.int32)
    run = passed[:, LANES:].astype(jnp.int32)
    dy = run % SIDE
    dz = (run // SIDE + (dy > y).astype(jnp.int32)) % rows
    slot = (dy * rows + dz) * 8 + within % 8
    slots = devices * 8
    hot_ref[...] = (
        (jnp.concatenate([slot] * (slots // LANES), axis=1) == iota((points, slots), 1))
        .astype(F32)
        .astype(BF16)
    )

    lower = (iota(square, 1) <= iota(square, 0)).astype(F32).astype(BF16)
    ends_col = dot(lower, counts_col.astype(BF16))
    passed_row = (
        (jnp.concatenate([ends_col] * (points // LANES), axis=1) <= iota((devices, points), 1).astype(F32))
        .astype(F32)
        .astype(BF16)
    )
    starts_row = dot(jnp.broadcast_to(counts, (8, devices)).astype(BF16), passed_row)[0:1]
    quarter_row = (iota((1, points), 1).astype(F32) - starts_row).astype(jnp.int32) // 8
    pair = jnp.concatenate([parts[0], parts[1]], axis=0).astype(F32)
    keep = quarter_row == iota((4 * 2 * RANK, points), 0) // (2 * RANK)
    spaced = jnp.where(keep, jnp.concatenate([pair] * 4, axis=0), 0.0).astype(BF16)
    spaced = dot(spaced, hot_ref[...]).T.astype(BF16)
    weight_out[...] = spaced.reshape(SIDE, slots // SIDE, LANES)

    for k in far:
        pltpu.make_async_remote_copy(
            weight_out.at[k], weight_in.at[k], weight_send, weight_recv,
            device_id=(at(0, SIDE - k), panel), device_id_type=MESH,
        ).start()
    weight_in[0] = weight_out[0]

    wide = jnp.concatenate([p for p in parts for _ in range(8)], axis=0)
    gram = dot_t(weights3, wide)
    gram = gram[0:RANK] + gram[RANK : 2 * RANK] + gram[2 * RANK :]
    gram = gram[:, 0:LANES] + gram[:, LANES : 2 * LANES] + gram[:, 2 * LANES :]
    packed = pack2(gram)
    gram_out[...] = packed
    gram_in[rank_in] = packed

    for peer in mates:
        pltpu.make_async_remote_copy(
            gram_out, gram_in.at[rank_in], gram_send, gram_recv,
            device_id=(peer, panel), device_id_type=MESH,
        ).start()

    quarter_ref[...] = (within // 8 == iota((points, LANES), 1) // channels).astype(F32)

    others = pl.ds(1, SIDE - 1)
    pltpu.make_async_copy(weight_in.at[others], weight_in.at[others], weight_recv).wait()
    weights_in = weight_in[...].reshape(slots, LANES).astype(F32).T.astype(BF16)
    pltpu.make_async_copy(middle.at[others], middle.at[others], one_recv).wait()

    held = jnp.concatenate(
        [middle[:, k].astype(F32).reshape(rows * 8, LANES) for k in range(SIDE)], axis=0
    ).astype(BF16)
    moment = dot(weights_in, held)
    part = iota((2 * RANK, LANES), 1) // channels
    moment = sum(
        jnp.where(part == q, moment[q * 2 * RANK : (q + 1) * 2 * RANK], 0.0) for q in range(4)
    )
    moment = group_sum(moment[:RANK] + moment[RANK:], channels)
    part = iota((4, LANES), 1) // channels
    low = jnp.where(part == 0, moment[0:4], moment[4:8])
    high = jnp.where(part == 2, moment[8:12], moment[12:16])
    packed = jnp.where(part < 2, low, high)
    moment_out[...] = packed
    moment_in[rank_in] = packed

    for peer in mates:
        pltpu.make_async_remote_copy(
            moment_out, moment_in.at[rank_in], moment_send, moment_recv,
            device_id=(peer, panel), device_id_type=MESH,
        ).start()

    peers = pl.ds(0, group - 1)
    pltpu.make_async_copy(gram_in.at[peers], gram_in.at[peers], gram_recv).wait()
    sub = iota((RANK, LANES), 0)
    lane = iota((RANK, LANES), 1)
    tableau = jnp.where(
        lane < RANK, unpack2(jnp.sum(gram_in[...], axis=0)), (lane - RANK == sub).astype(F32)
    )
    for k in range(RANK - 1):
        ratio = tableau[:, k : k + 1] / tableau[k : k + 1, k : k + 1]
        tableau = tableau - jnp.where(sub > k, ratio * tableau[k : k + 1, :], 0.0)
    pivots = jnp.sum(jnp.where(lane == sub, tableau, 0.0), axis=1, keepdims=True)
    tableau = tableau * (1.0 / jnp.sqrt(pivots))
    factor_ref[0] = jnp.where(lane >= sub, tableau, 0.0)[:, :RANK]
    inverse = jnp.concatenate(split3(tableau[:, RANK : 2 * RANK]), axis=0)

    two = [
        pltpu.make_async_remote_copy(
            middle.at[:, k], recv.at[k], two_send, two_recv,
            device_id=(at(0, k), panel), device_id_type=MESH,
        )
        for k in far
    ]
    for copy in two:
        copy.start()
    recv[0] = middle[:, 0]

    pltpu.make_async_copy(moment_in.at[peers], moment_in.at[peers], moment_recv).wait()
    packed = jnp.sum(moment_in[...], axis=0)
    moment = jnp.concatenate(
        [packed[:, q * channels : (q + 1) * channels] for q in range(4)], axis=0
    )
    coeffs = sum(dot(inverse, term) for term in split3(moment))
    coeffs = coeffs[0:RANK] + coeffs[RANK : 2 * RANK] + coeffs[2 * RANK :]
    coeffs_ref[0] = coeffs
    terms = split3(coeffs)
    gram = dot_t(
        jnp.concatenate(terms, axis=0),
        jnp.concatenate([p for p in terms for _ in range(8)], axis=0),
    )
    gram = gram[0:RANK] + gram[RANK : 2 * RANK] + gram[2 * RANK :]
    packed = pack2(gram[:, 0:LANES] + gram[:, LANES : 2 * LANES] + gram[:, 2 * LANES :])
    top_out[...] = packed
    top_in[panel] = packed

    for k in sorted(range(1, panels), key=lambda k: -min(k, panels - k)):
        pltpu.make_async_remote_copy(
            top_out, top_in.at[panel], top_send, top_recv,
            device_id=(me, lax.rem(panel + k, panels)), device_id_type=MESH,
        ).start()

    pltpu.make_async_copy(recv.at[others], recv.at[others], two_recv).wait()

    received = recv[...].astype(F32).reshape(slots, LANES).astype(BF16)
    relaid = dot(hot_ref[...], received)
    relaid = jnp.where(quarter_ref[...] > 0.5, relaid, 0.0).astype(BF16)

    fold = (iota((channels, LANES), 1) % channels == iota((channels, LANES), 0)).astype(F32).astype(BF16)
    for n in range(leaves):
        columns = dot_t(fold, relaid[n * LEAF : (n + 1) * LEAF]).astype(BF16)
        own[n] = columns
        ext[n + REACH] = columns
    right = lax.rem(me + 1, devices)
    left = lax.rem(me + devices - 1, devices)
    to_left = pltpu.make_async_remote_copy(
        own.at[pl.ds(0, REACH)], ext.at[pl.ds(leaves + REACH, REACH)], left_send, left_recv,
        device_id=(left, panel), device_id_type=MESH,
    )
    to_right = pltpu.make_async_remote_copy(
        own.at[pl.ds(leaves - REACH, REACH)], ext.at[pl.ds(0, REACH)], right_send, right_recv,
        device_id=(right, panel), device_id_type=MESH,
    )
    has_left = me > 0
    has_right = me < devices - 1

    @pl.when(has_left)
    def _():
        to_left.start()

    @pl.when(has_right)
    def _():
        to_right.start()

    @pl.when(me == 0)
    def _():
        ext[pl.ds(0, REACH)] = jnp.zeros((REACH, channels, LEAF), BF16)

    @pl.when(me == devices - 1)
    def _():
        ext[pl.ds(leaves + REACH, REACH)] = jnp.zeros((REACH, channels, LEAF), BF16)


    load_cols.wait()
    load_scales.wait()
    load_mats.wait()

    def near_leaf(i, source, first):
        rows = jnp.concatenate(
            [source[jnp.clip(cols_ref[NEAR * i + t] - first, 0, source.shape[0] - 1)] for t in range(NEAR)],
            axis=0,
        )
        width = NEAR * LEAF
        prod = dot(rows, mats[:, i * width : (i + 1) * width])
        lower = iota((channels, LANES), 1) < LEAF
        halves = []
        for h in range(2):
            cut = prod[:, h * LANES : (h + 1) * LANES]
            halves.append(
                jnp.where(
                    lower,
                    cut[2 * h * channels : (2 * h + 1) * channels] * scales_ref[NEAR * i + 2 * h],
                    cut[(2 * h + 1) * channels : (2 * h + 2) * channels] * scales_ref[NEAR * i + 2 * h + 1],
                )
            )
        both = halves[0] + halves[1]
        return both + pltpu.roll(both, LEAF, 1)

    def near_pair(i, source, first):
        a = near_leaf(i, source, first)
        b = near_leaf(i + 1, source, first)
        lower = iota((channels, LANES), 1) < LEAF
        near_ref[:, i * LEAF : (i + 2) * LEAF] = jnp.where(lower, a, b).astype(BF16)

    for i in range(REACH, leaves - REACH, 2):
        near_pair(i, own, me * leaves)

    @pl.when(has_right)
    def _():
        to_left.wait_recv()

    @pl.when(has_left)
    def _():
        to_right.wait_recv()

    first = me * leaves - REACH
    near_pair(0, ext, first)
    near_pair(leaves - 2, ext, first)

    peers = pl.ds(0, panels - 1)
    pltpu.make_async_copy(top_in.at[peers], top_in.at[peers], top_recv).wait()
    topgram_ref[0] = unpack2(jnp.sum(top_in[...], axis=0))[:, :RANK]

    pltpu.make_async_copy(out.at[others], out.at[others], one_send).wait()
    pltpu.make_async_copy(weight_in.at[others], weight_in.at[others], weight_send).wait()
    pltpu.make_async_copy(recv.at[others], recv.at[others], two_send).wait()
    peers = pl.ds(0, group - 1)
    pltpu.make_async_copy(gram_in.at[peers], gram_in.at[peers], gram_send).wait()
    pltpu.make_async_copy(moment_in.at[peers], moment_in.at[peers], moment_send).wait()
    peers = pl.ds(0, panels - 1)
    pltpu.make_async_copy(top_in.at[peers], top_in.at[peers], top_send).wait()
    @pl.when(has_left)
    def _():
        to_left.wait_send()

    @pl.when(has_right)
    def _():
        to_right.wait_send()


def on_device(
    inputs, local_order, run_counts, near_cols, near_blocks, near_scales, leaf_bases, local_tiles,
    cross_tiles,
):
    devices = lax.axis_size("cluster")
    panels = lax.axis_size("panel")
    channels, points = inputs.shape
    leaves = points // LEAF
    group = 2**CROSS
    vmem = pl.BlockSpec(memory_space=pltpu.VMEM)
    hbm = pl.BlockSpec(memory_space=pl.ANY)
    dma = pltpu.SemaphoreType.DMA
    operands = (
        inputs,
        local_order.reshape(points // LANES, LANES),
        run_counts,
        run_counts.reshape(1, devices),
        near_cols,
        near_scales,
        near_blocks,
        leaf_bases,
        jnp.transpose(local_tiles, (1, 2, 0)),
        jnp.transpose(cross_tiles, (1, 2, 0)),
    )
    operands = [pltpu.with_memory_space_constraint(x, pltpu.HBM) for x in operands]
    spaces = [pltpu.VMEM, pltpu.VMEM, pltpu.SMEM, pltpu.VMEM, pltpu.SMEM, pltpu.SMEM] + [pltpu.VMEM] * 4
    slots = (SIDE, SIDE, 8, LANES)
    shapes = (
        ((channels, points), BF16),
        ((1, RANK, channels), F32),
        ((1, RANK, RANK), F32),
        ((1, RANK, RANK), F32),
    )
    results = pl.pallas_call(
        functools.partial(body, devices, panels),
        out_shape=tuple(pltpu.VMEM(*s) for s in shapes),
        in_specs=[hbm] * len(operands),
        out_specs=(vmem,) * 4,
        scratch_shapes=[space(x.shape, x.dtype) for space, x in zip(spaces, operands)]
        + [
            pltpu.VMEM((points + CAP, LANES), F32),
            pltpu.VMEM(slots, BF16),
            pltpu.VMEM(slots, BF16),
            pltpu.VMEM(slots, BF16),
            pltpu.VMEM((SIDE, devices * 8 // SIDE, LANES), BF16),
            pltpu.VMEM((SIDE, devices * 8 // SIDE, LANES), BF16),
            pltpu.VMEM((leaves, channels, LEAF), BF16),
            pltpu.VMEM((leaves + 2 * REACH, channels, LEAF), BF16),
            pltpu.VMEM((4, LANES), F32),
            pltpu.VMEM((group, 4, LANES), F32),
            pltpu.VMEM((2, LANES), F32),
            pltpu.VMEM((group, 2, LANES), F32),
            pltpu.VMEM((2, LANES), F32),
            pltpu.VMEM((panels, 2, LANES), F32),
            pltpu.VMEM((points, devices * 8), BF16),
            pltpu.VMEM((points, LANES), F32),
            dma((len(operands),)),
        ]
        + [dma] * 16,
        compiler_params=pltpu.CompilerParams(
            collective_id=0, has_side_effects=True, vmem_limit_bytes=48 * 2**20
        ),
    )(*operands)
    return pl.pallas_call(
        store,
        out_shape=tuple(jax.ShapeDtypeStruct(*s) for s in shapes),
        in_specs=[hbm] * 4,
        out_specs=(hbm,) * 4,
        scratch_shapes=[dma((4,))],
    )(*[pltpu.with_memory_space_constraint(x, pltpu.VMEM) for x in results])


def store(*refs):
    sems = refs[8]
    copies = [pltpu.make_async_copy(refs[k], refs[4 + k], sems.at[k]) for k in range(4)]
    for copy in copies:
        copy.start()
    for copy in copies:
        copy.wait()


def solution(mesh):
    placed = (
        P("panel", "cluster"),
        P("cluster"),
        P(),
        P("cluster"),
        P(None, "cluster"),
        P("cluster"),
        P(None, "cluster"),
        P("cluster", None, None),
        P(),
    )
    return jax.shard_map(
        on_device,
        mesh=mesh,
        in_specs=placed,
        out_specs=(
            P("panel", "cluster"),
            P("cluster", None, "panel"),
            P("cluster", None, None),
            P("cluster", None, None),
        ),
        check_vma=False,
    )
```
